32 devices in a mesh: sky: 16 (over z, y, core), exp: 2 (over x).
Axes of the slice: x: 2, y: 2, z: 4, core: 2. Of those that a mesh axis runs over, the one named last changes fastest.
Arguments:
- warped: bfloat16 [4, 1920, 1024], P('exp', 'sky'), may hold values from -6 to 6
- variance: bfloat16 [4, 1920, 1024], P('exp', 'sky'), may hold values from 0.5 to 8
- basis_taps: bfloat16 [9, 2, 23], replicated, may hold values from -1.25 to 1.25
- coeffs: float32 [4, 9, 10], P('exp'), may hold values from -6 to 6
- degrees: int32 [4, 9], P('exp'), may hold values from 0 to 3
- footprint: int32 [4, 2], P('exp'), may hold values from 0 to 1920, as said below
- masks: int32 [4, 128], P('exp', 'sky'), may hold values from 0 to 1073741823
Outputs:
- coadd: float32 [1920, 1024], P('sky', 'exp')
The draws below stay inside these ranges and needn't reach their ends.
Inputs may be any that keep to these rules, and one draw needn't show every extreme that they name: Each exposure covers rows footprint[e, 0] up to but not including footprint[e, 1], a nonempty range.
All inputs are finite; a program needn't handle non-finite values.
Results may differ from the reference program's by a relative error of at most 0.0039.
Values may be sent and summed in bfloat16 or wider, within the bound.
No kernel may reach another device: no remote copies, remote signals or barrier semaphores. Data moves between devices by JAX's collectives and lax.ppermute only.
A program may use at most 64 MiB of HBM per device.

```python
import math
import jax
import jax.numpy as jnp
from jax import lax

COLS = 1024
NB = 9
KW = 23
NTERM = 10
HALF = 11
NE = 4
NR = 1920


def draw_footprint(key, part):
    first_key, second_key = jax.random.split(jax.random.fold_in(key, 17))
    lower = jnp.maximum(jax.random.randint(first_key, (NE,), -(NR // 4), NR // 2), 0)
    upper = jnp.minimum(lower + jax.random.randint(second_key, (NE,), NR // 4, NR + 1), NR)
    return jnp.stack([lower, upper], axis=1).astype(jnp.int32)


def set_ends(result, rng, low, largest):
    longest = result.shape.index(max(result.shape))
    spots = []
    for shift in (0, 1):
        where = [jax.random.randint(jax.random.fold_in(rng, axis), (), 0, length) for axis, length in enumerate(result.shape)]
        where[longest] = (where[longest] + shift) % result.shape[longest]
        spots.append(tuple(where))
    return result.at[spots[0]].set(low).at[spots[1]].set(largest)


def level_of(key, extent, pieces, least, top_value):
    gain = 1.0
    for axis_at, blocks in pieces:
        heights = jax.random.uniform(jax.random.fold_in(jax.random.fold_in(key, 6), axis_at), (blocks,), jnp.float32, least / len(pieces), top_value / len(pieces))
        gain = gain * jnp.repeat(jnp.exp(heights), extent[axis_at] // blocks).reshape((-1,) + (1,) * (len(extent) - 1 - axis_at))
    return gain


def centred(stream_key, shape, deviation, reach, pieces=(), kind=jnp.bfloat16):
    result = deviation * jax.random.normal(stream_key, shape, jnp.float32)
    if pieces:
        result = result * level_of(stream_key, shape, pieces, -0.22, 0.18)
    return jnp.clip(result, -reach, reach).astype(kind)


def setup_inputs(seed: int = 0) -> dict:
    seeds = jax.random.split(jax.random.key(seed), 8)
    return {
        "warped": centred(seeds[0], (NE, NR, COLS), 1.0, 6.0, ((0, 2), (1, 16))),
        "variance": jnp.clip(jnp.exp(math.log(8.0) - 2.7725887 * jax.random.uniform(seeds[1], (NE, NR, COLS), jnp.float32) ** level_of(seeds[1], (NE, NR, COLS), ((0, 2), (1, 16)), -0.2, 0.2)), 0.5, 8.0).astype(jnp.bfloat16),
        "basis_taps": centred(seeds[2], (NB, 2, KW), KW ** -0.5, 1.25),
        "coeffs": centred(seeds[3], (NE, NB, NTERM), 0.4, 6.0, ((0, 2),), jnp.float32),
        "degrees": set_ends(jax.random.randint(seeds[4], (NE, NB), 0, 4), jax.random.fold_in(seeds[4], 1), 0, 3).astype(jnp.int32),
        "footprint": draw_footprint(jax.random.fold_in(seeds[7], 71), 0),
        "masks": set_ends(jax.random.randint(seeds[6], (NE, NR // 15), 0, 1073741824), jax.random.fold_in(seeds[6], 1), 0, 1073741823).astype(jnp.int32),
    }


HIGHEST = lax.Precision.HIGHEST
POWERS = ((0, 0), (1, 0), (0, 1), (2, 0), (1, 1), (0, 2), (3, 0), (2, 1), (1, 2), (0, 3))


def monomials(total_rows, total_cols, row_start, row_count):
    row_pos = (2.0 * (row_start + jnp.arange(row_count, dtype=jnp.int32)).astype(jnp.float32) + 1.0) / total_rows - 1.0
    col_pos = (2.0 * jnp.arange(total_cols, dtype=jnp.int32).astype(jnp.float32) + 1.0) / total_cols - 1.0
    return jnp.stack([(row_pos ** p)[:, None] * (col_pos ** q)[None, :] for p, q in POWERS])


def term_active(degree):
    orders = jnp.array([p + q for p, q in POWERS], dtype=jnp.int32)
    return (orders[None, :] <= degree[:, None]).astype(jnp.float32)


def pixel_weight(bounds, words, var_field, global_rows, local_rows):
    covered = ((global_rows >= bounds[0]) & (global_rows < bounds[1])).astype(jnp.float32)
    per_row = jnp.repeat(words, 15, total_repeat_length=local_rows.shape[0])
    offset = 2 * (local_rows % 15)
    lower = jnp.right_shift(per_row, offset) & 1
    upper = jnp.right_shift(per_row, offset + 1) & 1
    usable = (1 - lower * upper).astype(jnp.float32)
    return (covered * usable)[:, None] / var_field.astype(jnp.float32)


def reference(warped, variance, basis_taps, coeffs, degrees, footprint, masks):
    tap_values = basis_taps.astype(jnp.float32)
    row_kernel = tap_values[:, 0, :].reshape(NB, 1, KW, 1)
    col_kernel = tap_values[:, 1, :].reshape(NB, 1, 1, KW)
    terms_field = monomials(NR, COLS, 0, NR)
    row_index = jnp.arange(NR, dtype=jnp.int32)
    layout = ("NCHW", "OIHW", "NCHW")

    def first_pass(carry, item):
        image, coef, degree, bounds, words, var_field = item
        source = image.astype(jnp.float32).reshape(1, 1, NR, COLS)
        along_rows = lax.conv_general_dilated(source, row_kernel, (1, 1), ((HALF, HALF), (0, 0)), dimension_numbers=layout, precision=HIGHEST)
        along_rows = lax.optimization_barrier(along_rows.astype(jnp.bfloat16)).astype(jnp.float32)
        along_cols = lax.conv_general_dilated(along_rows, col_kernel, (1, 1), ((0, 0), (HALF, HALF)), dimension_numbers=layout, feature_group_count=NB, precision=HIGHEST)[0]
        field = jnp.einsum("bt,trc->brc", coef * term_active(degree), terms_field, precision=HIGHEST)
        matched = jnp.sum(field * along_cols, axis=0).astype(jnp.bfloat16)
        weight = pixel_weight(bounds, words, var_field, row_index, row_index)
        values = matched.astype(jnp.float32)
        return (carry[0] + weight * values, carry[1] + weight), matched

    start = (jnp.zeros((NR, COLS), jnp.float32), jnp.zeros((NR, COLS), jnp.float32))
    (num_first, den_first), matched_all = lax.scan(first_pass, start, (warped, coeffs, degrees, footprint, masks, variance))
    first = num_first / (1.0 + den_first)

    def second_pass(carry, item):
        matched, bounds, words, var_field = item
        weight = pixel_weight(bounds, words, var_field, row_index, row_index)
        values = matched.astype(jnp.float32)
        excess = values - first
        robust = weight / (1.0 + excess * excess / (9.0 * var_field.astype(jnp.float32)))
        return (carry[0] + robust * values, carry[1] + robust), None

    (num_final, den_final), unused = lax.scan(second_pass, start, (matched_all, footprint, masks, variance))
    return num_final / (1.0 + den_final)
```

```python
import functools

import jax
import jax.numpy as jnp
from jax import lax
from jax.experimental import pallas as pl
from jax.experimental.pallas import tpu as pltpu
from jax.sharding import PartitionSpec as P

POWERS = ((0, 0), (1, 0), (0, 1), (2, 0), (1, 1), (0, 2), (3, 0), (2, 1), (1, 2), (0, 3))
TERM = {power: index for index, power in enumerate(POWERS)}
ROWS_PER_WORD = 15
EDGE = 16
WINDOW = 256
LANES = 128
PAD = 64
F32 = jnp.float32
BF16 = jnp.bfloat16


def round_up(value, unit):
    return -(-value // unit) * unit


def prep_kernel(width, shares, place, footprint, masks, variance, warped, tail, head, *masked):
    exp_count, row_count, col_count = variance.shape
    words = masks.shape[1]
    local = lax.broadcasted_iota(jnp.int32, (row_count, LANES), 0)
    total = local + place[0]
    for e in range(exp_count):
        image = warped[e].astype(F32)
        tail[e] = image[row_count - EDGE :].astype(BF16)
        head[e] = image[:EDGE].astype(BF16)
        word = jnp.full((row_count, LANES), masks[e, 0], jnp.int32)
        first = jnp.zeros((row_count, LANES), jnp.int32)
        for w in range(1, words):
            here = local >= w * ROWS_PER_WORD
            word = jnp.where(here, masks[e, w], word)
            first = jnp.where(here, w * ROWS_PER_WORD, first)
        planes = lax.shift_right_logical(word, 2 * (local - first)) & 3
        counts = (total >= footprint[e, 0]) & (total < footprint[e, 1]) & (planes != 3)
        for k in range(shares):
            start = pl.multiple_of(place[1 + k], LANES)
            for j in range(width // LANES):
                block = variance[e, :, pl.ds(pl.multiple_of(start + j * LANES, LANES), LANES)].astype(F32)
                masked[k][e, :, j * LANES : (j + 1) * LANES] = jnp.where(counts, block, jnp.inf).astype(BF16)


def band_kernel(taps, row_band, col_band):
    basis_count, _, tap_count = taps.shape
    half = tap_count // 2
    for b in range(basis_count):
        both = taps[b].astype(F32)
        both = jnp.concatenate([both, jnp.zeros((2, WINDOW - tap_count), F32)], axis=1)
        row_line = jnp.broadcast_to(pltpu.roll(both, WINDOW - half, 1)[0:1], (LANES, WINDOW))
        col_line = jnp.broadcast_to(pltpu.roll(both, PAD - half, 1)[1:2], (LANES, WINDOW))
        row_band[b] = pltpu.roll(row_line, 0, 1, stride=1, stride_axis=0).astype(BF16)
        col_band[b] = pltpu.roll(col_line, 0, 1, stride=1, stride_axis=0).T.astype(BF16)


def match_kernel(share, total_rows, place, coeffs, degrees, warped, above, below, row_band, col_band, matched, strip, rows, total):
    exp_count, row_count, col_count = warped.shape
    basis_count = row_band.shape[0]
    width = matched.shape[2]
    blocks = width // LANES
    start = pl.multiple_of(place[1 + share], LANES)
    left_at = pl.multiple_of(jnp.maximum(start - LANES, 0), LANES)
    right_at = pl.multiple_of(jnp.minimum(start + width, col_count - LANES), LANES)
    has_left = start > 0
    has_right = start + width < col_count

    def rows_of(e, at, size):
        middle = warped[e, :, pl.ds(at, size)].astype(F32)
        up = above[e, :, pl.ds(at, size)].astype(F32)
        down = below[e, :, pl.ds(at, size)].astype(F32)
        gap = jnp.zeros((WINDOW - row_count - 2 * EDGE, size), F32)
        return jnp.concatenate([middle, down, gap, up], axis=0)

    for e in range(exp_count):
        left = jnp.where(has_left, rows_of(e, left_at, LANES), 0.0)
        right = jnp.where(has_right, rows_of(e, right_at, LANES), 0.0)
        wide = jnp.concatenate([left, rows_of(e, start, width), right], axis=1)
        strip[e] = wide[:, PAD : PAD + width + LANES].astype(BF16)

    band = row_band[...].reshape(basis_count * LANES, WINDOW)
    for e in range(exp_count):
        rows[e] = jnp.dot(band, strip[e], preferred_element_type=F32).astype(BF16)

    row_at = place[0] + lax.broadcasted_iota(jnp.int32, (row_count, LANES), 0)
    u = (2.0 * row_at.astype(F32) + 1.0) / total_rows - 1.0
    total[...] = jnp.zeros_like(total)

    def one_basis(b, carry):
        columns = col_band[b]
        at = pl.multiple_of(b * LANES, LANES)
        for e in range(exp_count):
            degree = degrees[e, b]

            def term(p, q):
                return jnp.where(degree >= p + q, coeffs[e, b, TERM[p, q]], 0.0)

            a0 = term(0, 0) + u * (term(1, 0) + u * (term(2, 0) + u * term(3, 0)))
            a1 = term(0, 1) + u * (term(1, 1) + u * term(2, 1))
            a2 = term(0, 2) + u * term(1, 2)
            a3 = term(0, 3)
            for j in range(blocks):
                window = rows[e, pl.ds(at, LANES), j * LANES : j * LANES + WINDOW]
                along = jnp.dot(window, columns, preferred_element_type=F32)[:row_count]
                col_at = start + j * LANES + lax.broadcasted_iota(jnp.int32, (1, LANES), 1)
                v = (2.0 * col_at.astype(F32) + 1.0) / col_count - 1.0
                field = a0 + v * (a1 + v * (a2 + v * a3))
                total[e, :, j * LANES : (j + 1) * LANES] += field * along
        return carry

    lax.fori_loop(0, basis_count, one_basis, 0)
    matched[...] = total[...].astype(BF16)


def coadd_kernel(shares, *refs):
    fields, variances, coadd = refs[:shares], refs[shares : 2 * shares], refs[2 * shares]
    exp_count, row_count, width = fields[0].shape
    for j in range(width // LANES):
        span = slice(j * LANES, (j + 1) * LANES)
        values = [f[e, :, span].astype(F32) for f in fields for e in range(exp_count)]
        spreads = [s[e, :, span].astype(F32) for s in variances for e in range(exp_count)]
        weights = [1.0 / s for s in spreads]
        first = sum(w * x for w, x in zip(weights, values)) / (1.0 + sum(weights))
        robust = [1.0 / (s + (x - first) * (x - first) * (1.0 / 9.0)) for s, x in zip(spreads, values)]
        coadd[:, span] = sum(r * x for r, x in zip(robust, values)) / (1.0 + sum(robust))


def body(warped, variance, basis_taps, coeffs, degrees, footprint, masks):
    exp_count, row_count, col_count = warped.shape
    basis_count, _, tap_count = basis_taps.shape
    sky_count, shares = lax.axis_size("sky"), lax.axis_size("exp")
    width = col_count // shares
    total_rows = row_count * sky_count
    mine = lax.axis_index("exp")
    place = jnp.stack(
        [lax.axis_index("sky") * row_count] + [lax.rem(mine + k, shares) * width for k in range(shares)]
    ).astype(jnp.int32)
    smem = pl.BlockSpec(memory_space=pltpu.SMEM)
    vmem = pl.BlockSpec(memory_space=pltpu.VMEM)
    edge = jax.ShapeDtypeStruct((exp_count, EDGE, col_count), BF16)
    share = jax.ShapeDtypeStruct((exp_count, row_count, width), BF16)

    tail, head, *masked = pl.pallas_call(
        functools.partial(prep_kernel, width, shares),
        out_shape=[edge, edge] + [share] * shares,
        in_specs=[smem, smem, smem, vmem, vmem],
        out_specs=[vmem] * (2 + shares),
        name="prep",
    )(place, footprint, masks, variance, warped)

    def to_share(values, k):
        return lax.ppermute(values, "exp", [(i, (i + k) % shares) for i in range(shares)])

    spreads = [masked[0]] + [to_share(masked[k], k) for k in range(1, shares)]
    above = lax.ppermute(tail, "sky", [(i, i + 1) for i in range(sky_count - 1)])
    below = lax.ppermute(head, "sky", [(i + 1, i) for i in range(sky_count - 1)])

    row_band, col_band = pl.pallas_call(
        band_kernel,
        out_shape=[
            jax.ShapeDtypeStruct((basis_count, LANES, WINDOW), BF16),
            jax.ShapeDtypeStruct((basis_count, WINDOW, LANES), BF16),
        ],
        in_specs=[vmem],
        out_specs=[vmem, vmem],
        name="bands",
    )(basis_taps)

    def match(k):
        return pl.pallas_call(
            functools.partial(match_kernel, k, total_rows),
            out_shape=share,
            in_specs=[smem, smem, smem] + [vmem] * 5,
            out_specs=vmem,
            scratch_shapes=[
                pltpu.VMEM((exp_count, WINDOW, width + LANES), BF16),
                pltpu.VMEM((exp_count, basis_count * LANES, width + LANES), BF16),
                pltpu.VMEM((exp_count, row_count, width), F32),
            ],
            name="match",
        )(place, coeffs, degrees, warped, above, below, row_band, col_band)

    fields = [None] + [to_share(match(k), k) for k in range(1, shares)]
    fields[0] = match(0)

    return pl.pallas_call(
        functools.partial(coadd_kernel, shares),
        out_shape=jax.ShapeDtypeStruct((row_count, width), F32),
        in_specs=[vmem] * (2 * shares),
        out_specs=vmem,
        name="coadd",
    )(*fields, *spreads)


def solution(mesh):
    in_specs = (
        P("exp", "sky", None),
        P("exp", "sky", None),
        P(),
        P("exp", None, None),
        P("exp", None),
        P("exp", None),
        P("exp", "sky"),
    )
    return jax.shard_map(body, mesh=mesh, in_specs=in_specs, out_specs=P("sky", "exp"), check_vma=False)
```

```python
import functools

import jax
import jax.numpy as jnp
from jax import lax
from jax.experimental import pallas as pl
from jax.experimental.pallas import tpu as pltpu
from jax.sharding import PartitionSpec as P

POWERS = ((0, 0), (1, 0), (0, 1), (2, 0), (1, 1), (0, 2), (3, 0), (2, 1), (1, 2), (0, 3))
TERM = {power: index for index, power in enumerate(POWERS)}
ROWS_PER_WORD = 15
EDGE = 16
LANES = 128
GROUP = 1
F32 = jnp.float32
BF16 = jnp.bfloat16


def round_up(value, unit):
    return -(-value // unit) * unit


def segments(width, tap_count):
    valid = LANES - tap_count + 1
    return [(at, min(valid, width - at)) for at in range(0, width, valid)]


def share_start(k, shares, width):
    return pl.multiple_of(lax.rem(lax.axis_index("exp") + k, shares) * width, LANES)


def variance_kernel(variance, *parts):
    shares, width = len(parts), parts[0].shape[2]
    for k in range(shares):
        parts[k][...] = variance[:, :, pl.ds(share_start(k, shares, width), width)]


def edges_kernel(warped, near, far):
    row_count = warped.shape[1]
    even = lax.rem(lax.axis_index("sky"), 2) == 0
    for e in range(warped.shape[0]):
        image = warped[e].astype(F32)
        head, tail = image[:EDGE], image[row_count - EDGE :]
        near[e] = jnp.where(even, tail, head).astype(BF16)
        far[e] = jnp.where(even, head, tail).astype(BF16)


def setup_kernel(taps, coeffs, degrees, footprint, masks, inner_band, outer_band, col_band, active, covered):
    basis_count, _, tap_count = taps.shape
    exp_count, row_count, _ = covered.shape
    half = tap_count // 2
    inner = inner_band.shape[1]

    both = jnp.concatenate([taps[b].astype(F32) for b in range(basis_count)], axis=0)
    lines = jnp.concatenate([both, jnp.zeros((2 * basis_count, LANES - tap_count), F32)], axis=1).astype(BF16)
    lane = lax.broadcasted_iota(jnp.int32, (LANES, LANES), 1)
    tap = lax.broadcasted_iota(jnp.int32, (LANES, LANES), 0)
    flip = (lane + tap == LANES).astype(F32) + ((lane == 0) & (tap == 0)).astype(F32)
    flipped = jnp.dot(lines, flip.astype(BF16), preferred_element_type=F32)
    lines = lines.astype(F32)

    def circulant(line, size):
        return pltpu.roll(jnp.broadcast_to(line, (size, LANES)), 0, 1, stride=1, stride_axis=0)

    near = pltpu.roll(lines, EDGE - half, 1)
    far = pltpu.roll(lines, LANES - 2 * EDGE - half, 1)
    for b in range(basis_count):
        upper = circulant(near[2 * b : 2 * b + 1], inner)
        lower = circulant(far[2 * b : 2 * b + 1], EDGE)
        inner_band[b] = upper.astype(BF16)
        outer_band[b] = jnp.concatenate([upper[:EDGE], lower], axis=0).astype(BF16)
        col_band[b] = circulant(flipped[2 * b + 1 : 2 * b + 2], LANES).astype(BF16)

    term_count = coeffs.shape[2]
    term = lax.broadcasted_iota(jnp.int32, (1, term_count), 1)
    order = jnp.zeros((1, term_count), F32)
    for index, (p, q) in enumerate(POWERS):
        order = jnp.where(term == index, float(p + q), order)
    wide = jnp.concatenate([degrees[...].astype(F32), jnp.zeros((exp_count, LANES - basis_count), F32)], axis=1)
    by_basis = jnp.concatenate([wide, jnp.zeros((8 - exp_count, LANES), F32)], axis=0).T
    local = lax.broadcasted_iota(jnp.int32, (row_count, LANES), 0)
    total = local + lax.axis_index("sky") * row_count
    for e in range(exp_count):
        own = jnp.concatenate([coeffs[b, e : e + 1, :] for b in range(basis_count)], axis=0)
        kept = jnp.where(order <= by_basis[:basis_count, e : e + 1], own, 0.0)
        kept = jnp.concatenate([kept, jnp.zeros((16 - basis_count, term_count), F32)], axis=0)
        active[e] = jnp.concatenate([kept, jnp.zeros((16, LANES - term_count), F32)], axis=1)
        word = jnp.broadcast_to(masks[e : e + 1, 0:1], (row_count, LANES))
        first = jnp.zeros((row_count, LANES), jnp.int32)
        for w in range(1, masks.shape[1]):
            here = local >= w * ROWS_PER_WORD
            word = jnp.where(here, jnp.broadcast_to(masks[e : e + 1, w : w + 1], (row_count, LANES)), word)
            first = jnp.where(here, w * ROWS_PER_WORD, first)
        planes = lax.shift_right_logical(word, 2 * (local - first)) & 3
        low = jnp.broadcast_to(footprint[e : e + 1, 0:1], (row_count, LANES))
        high = jnp.broadcast_to(footprint[e : e + 1, 1:2], (row_count, LANES))
        covered[e] = ((total >= low) & (total < high) & (planes != 3)).astype(F32)


def windows_of(read, start, width, col_count, parts, half):
    left_at = pl.multiple_of(jnp.maximum(start - LANES, 0), LANES)
    right_at = pl.multiple_of(jnp.minimum(start + width, col_count - LANES), LANES)
    left = jnp.where(start > 0, read(left_at, LANES), 0.0)
    right = jnp.where(start + width < col_count, read(right_at, LANES), 0.0)
    middle = read(start, width)
    blocks = [left] + [middle[:, at : at + LANES] for at in range(0, width, LANES)] + [right]
    blocks = [pltpu.roll(block, half, 1) for block in blocks]
    lane = lax.broadcasted_iota(jnp.int32, left.shape, 1)
    place = jnp.where(lane >= half, lane - half, lane - half + LANES)
    pieces = []
    for at, _ in parts:
        base, offset = divmod(LANES + at - half, LANES)
        pieces.append(jnp.where(place >= offset, blocks[base], blocks[base + 1]))
    return jnp.concatenate(pieces, axis=1).astype(BF16)


def line_polynomials(active, lines, start, parts, col_count):
    exp_count = active.shape[0]
    for e in range(exp_count):
        values = active[e]

        def column(p, q):
            return jnp.broadcast_to(values[:, TERM[p, q] : TERM[p, q] + 1], values.shape)

        for s, (at, size) in enumerate(parts):
            lane = lax.broadcasted_iota(jnp.int32, values.shape, 1)
            col_at = at + jnp.where(lane >= at % LANES, lane - at % LANES, lane - at % LANES + LANES)
            v = (2.0 * (start + col_at).astype(F32) + 1.0) / col_count - 1.0
            span = slice(s * LANES, (s + 1) * LANES)
            lines[e, 0, :, span] = column(0, 0) + v * (column(0, 1) + v * (column(0, 2) + v * column(0, 3)))
            lines[e, 1, :, span] = column(1, 0) + v * (column(1, 1) + v * column(1, 2))
            lines[e, 2, :, span] = column(2, 0) + v * column(2, 1)
            lines[e, 3, :, span] = column(3, 0)


def weighted_sums(members, lines, rows, col_band, size, u):
    totals = [None] * len(members)
    for b in range(col_band.shape[0]):
        window = jnp.concatenate(
            [rows[e, b * size : (b + 1) * size, s * LANES : (s + 1) * LANES] for e, s in members], axis=0
        )
        along = jnp.dot(window, col_band[b], preferred_element_type=F32)
        for i, (e, s) in enumerate(members):
            r0, r1, r2, r3 = (lines[e, p, b : b + 1, s * LANES : (s + 1) * LANES] for p in range(4))
            value = (r0 + u * (r1 + u * (r2 + u * r3))) * along[i * size : (i + 1) * size]
            totals[i] = value if b == 0 else totals[i] + value
    return totals


def joined(blocks, parts, width):
    out = []
    for low in range(0, width, LANES):
        lane = low + lax.broadcasted_iota(jnp.int32, blocks[0].shape, 1)
        tile = None
        for block, (at, size) in zip(blocks, parts):
            if at < low + LANES and at + size > low:
                tile = block if tile is None else jnp.where(lane >= at, block, tile)
        out.append(tile)
    return jnp.concatenate(out, axis=1)


def row_position(first, rows, total_rows):
    row_at = first + lax.broadcasted_iota(jnp.int32, (rows, LANES), 0)
    return (2.0 * row_at.astype(F32) + 1.0) / total_rows - 1.0


def inner_kernel(k, shares, total_rows, half, warped, active, covered, inner_band, col_band, matched, strip, rows, lines):
    exp_count, row_count, col_count = warped.shape
    basis_count, size, _ = inner_band.shape
    _, inner, width = matched.shape
    parts = segments(width, 2 * half + 1)
    start = share_start(k, shares, width)
    u = row_position(lax.axis_index("sky") * row_count + EDGE, size, total_rows)
    line_polynomials(active, lines, start, parts, col_count)
    band = inner_band[...].reshape(basis_count * size, LANES)
    for e in range(exp_count):

        def read(at, count):
            own = warped[e, :, pl.ds(at, count)].astype(F32)
            return jnp.concatenate([own, jnp.zeros((LANES - row_count, count), F32)], axis=0)

        strip[e] = windows_of(read, start, width, col_count, parts, half)
        rows[e] = jnp.dot(band, strip[e], preferred_element_type=F32).astype(BF16)
    for e in range(exp_count):
        blocks = []
        for first in range(0, len(parts), GROUP):
            members = [(e, s) for s in range(first, min(first + GROUP, len(parts)))]
            blocks += weighted_sums(members, lines, rows, col_band, size, u)
        counts = jnp.concatenate([covered[e, EDGE : EDGE + inner]] * (width // LANES), axis=1) > 0
        matched[e] = jnp.where(counts, joined(blocks, parts, width)[:inner], jnp.inf).astype(BF16)


def outer_kernel(shares, total_rows, half, warped, near, far, active, covered, outer_band, col_band, *refs):
    matched, (strip, rows, lines) = refs[:shares], refs[shares:]
    exp_count, row_count, col_count = warped.shape
    basis_count, size, _ = outer_band.shape
    width = matched[0].shape[2]
    parts = segments(width, 2 * half + 1)
    span = LANES // 2 - EDGE
    sky = lax.axis_index("sky")
    even = lax.rem(sky, 2) == 0
    u = jnp.concatenate(
        [
            row_position(sky * row_count, EDGE, total_rows),
            row_position((sky + 1) * row_count - EDGE, EDGE, total_rows),
        ],
        axis=0,
    )
    band = outer_band[...].reshape(basis_count * size, LANES)
    for k in range(shares):
        start = share_start(k, shares, width)
        line_polynomials(active, lines.at[k], start, parts, col_count)
        for e in range(exp_count):

            def read(at, count):
                own = warped[e, :, pl.ds(at, count)].astype(F32)
                same = near[e, :, pl.ds(at, count)].astype(F32)
                other = far[e, :, pl.ds(at, count)].astype(F32)
                up, down = jnp.where(even, other, same), jnp.where(even, same, other)
                return jnp.concatenate([up, own[:span], own[row_count - span :], down], axis=0)

            strip[k, e] = windows_of(read, start, width, col_count, parts, half)
            rows[k, e] = jnp.dot(band, strip[k, e], preferred_element_type=F32).astype(BF16)
    for k in range(shares):
        members = [(e, s) for e in range(exp_count) for s in range(len(parts))]
        blocks = weighted_sums(members, lines.at[k], rows.at[k], col_band, size, u)
        for e in range(exp_count):
            own = blocks[e * len(parts) : (e + 1) * len(parts)]
            counts = jnp.concatenate([covered[e, :EDGE], covered[e, row_count - EDGE :]], axis=0)
            counts = jnp.concatenate([counts] * (width // LANES), axis=1) > 0
            matched[k][e] = jnp.where(counts, joined(own, parts, width), jnp.inf).astype(BF16)


def coadd_kernel(shares, *refs):
    inner, outer, variances, coadd = refs[:shares], refs[shares : 2 * shares], refs[2 * shares : 3 * shares], refs[-1]
    exp_count, row_count, width = variances[0].shape
    for j in range(width // LANES):
        span = slice(j * LANES, (j + 1) * LANES)
        values, spreads, weights = [], [], []
        for k in range(shares):
            for e in range(exp_count):
                edges = outer[k][e, :, span].astype(F32)
                value = jnp.concatenate([edges[:EDGE], inner[k][e, :, span].astype(F32), edges[EDGE:]], axis=0)
                counts = value < jnp.inf
                spread = jnp.where(counts, variances[k][e, :, span].astype(F32), jnp.inf)
                values.append(jnp.where(counts, value, 0.0))
                spreads.append(spread)
                weights.append(1.0 / spread)
        first = sum(w * x for w, x in zip(weights, values)) / (1.0 + sum(weights))
        robust = [1.0 / (s + (x - first) * (x - first) * (1.0 / 9.0)) for s, x in zip(spreads, values)]
        coadd[:, span] = sum(r * x for r, x in zip(robust, values)) / (1.0 + sum(robust))


def body(warped, variance, basis_taps, coeffs, degrees, footprint, masks):
    exp_count, row_count, col_count = warped.shape
    basis_count, _, tap_count = basis_taps.shape
    half = tap_count // 2
    sky_count, shares = lax.axis_size("sky"), lax.axis_size("exp")
    width = col_count // shares
    total_rows = row_count * sky_count
    inner = row_count - 2 * EDGE
    size = round_up(inner, 16)
    spans = len(segments(width, tap_count)) * LANES
    vmem = pl.BlockSpec(memory_space=pltpu.VMEM)

    def array(*shape, dtype=BF16):
        return jax.ShapeDtypeStruct(shape, dtype)

    def call(kernel, name, out_shape, *operands, scratch=(), mebibytes=8, cost=0.1):
        outputs = len(out_shape) if isinstance(out_shape, list) else 0
        return pl.pallas_call(
            kernel,
            out_shape=out_shape,
            in_specs=[vmem] * len(operands),
            out_specs=[vmem] * outputs if outputs else vmem,
            scratch_shapes=scratch,
            compiler_params=pltpu.CompilerParams(vmem_limit_bytes=mebibytes * 2**20),
            cost_estimate=pl.CostEstimate(flops=int(cost * 1e9), bytes_accessed=int(cost * 3e6), transcendentals=0),
            name=name,
        )(*operands)

    def to_share(values, k):
        return lax.ppermute(values, "exp", [(i, (i + k) % shares) for i in range(shares)])

    variances = call(variance_kernel, "variance", [array(exp_count, row_count, width)] * shares, variance)
    variances = [variances[0]] + [to_share(variances[k], k) for k in range(1, shares)]

    edge = array(exp_count, EDGE, col_count)
    near, far = call(edges_kernel, "edges", [edge, edge], warped)
    near = lax.ppermute(near, "sky", [(i, i ^ 1) for i in range(sky_count) if i ^ 1 < sky_count])
    pairs = [(i, i + 1) for i in range(1, sky_count - 1, 2)]
    far = lax.ppermute(far, "sky", pairs + [(j, i) for i, j in pairs])

    inner_band, outer_band, col_band, active, covered = call(
        setup_kernel,
        "setup",
        [
            array(basis_count, size, LANES),
            array(basis_count, 2 * EDGE, LANES),
            array(basis_count, LANES, LANES),
            array(exp_count, 16, LANES, dtype=F32),
            array(exp_count, row_count, LANES, dtype=F32),
        ],
        basis_taps,
        jnp.transpose(coeffs, (1, 0, 2)),
        degrees,
        footprint,
        masks,
        cost=0.6,
    )

    def inside(k):
        return call(
            functools.partial(inner_kernel, k, shares, total_rows, half),
            "inner",
            array(exp_count, inner, width),
            warped,
            active,
            covered,
            inner_band,
            col_band,
            scratch=[
                pltpu.VMEM((exp_count, LANES, spans), BF16),
                pltpu.VMEM((exp_count, basis_count * size, spans), BF16),
                pltpu.VMEM((exp_count, 4, 16, spans), F32),
            ],
            mebibytes=12,
            cost=2.0,
        )

    inners = [None] + [to_share(inside(k), k) for k in range(1, shares)]
    variances, near = lax.optimization_barrier((variances, near))
    outers = call(
        functools.partial(outer_kernel, shares, total_rows, half),
        "outer",
        [array(exp_count, 2 * EDGE, width)] * shares,
        warped,
        near,
        far,
        active,
        covered,
        outer_band,
        col_band,
        scratch=[
            pltpu.VMEM((shares, exp_count, LANES, spans), BF16),
            pltpu.VMEM((shares, exp_count, basis_count * 2 * EDGE, spans), BF16),
            pltpu.VMEM((shares, exp_count, 4, 16, spans), F32),
        ],
        mebibytes=12,
        cost=1.5,
    )
    outers = [outers[0]] + [to_share(outers[k], k) for k in range(1, shares)]
    inners[0] = inside(0)

    return call(
        functools.partial(coadd_kernel, shares),
        "coadd",
        array(row_count, width, dtype=F32),
        *inners,
        *outers,
        *variances,
        cost=0.5,
    )


def solution(mesh):
    in_specs = (
        P("exp", "sky", None),
        P("exp", "sky", None),
        P(),
        P("exp", None, None),
        P("exp", None),
        P("exp", None),
        P("exp", "sky"),
    )
    return jax.shard_map(body, mesh=mesh, in_specs=in_specs, out_specs=P("sky", "exp"), check_vma=False)
```

```python
import functools

import jax
import jax.numpy as jnp
from jax import lax
from jax.experimental import pallas as pl
from jax.experimental.pallas import tpu as pltpu
from jax.sharding import PartitionSpec as P

POWERS = ((0, 0), (1, 0), (0, 1), (2, 0), (1, 1), (0, 2), (3, 0), (2, 1), (1, 2), (0, 3))
TERM = {power: index for index, power in enumerate(POWERS)}
ROWS_PER_WORD = 15
EDGE = 16
LANES = 128
GROUP = 3
PIECES = 6
F32 = jnp.float32
BF16 = jnp.bfloat16


def round_up(value, unit):
    return -(-value // unit) * unit


def segments(width, tap_count):
    valid = LANES - tap_count + 1
    return [(at, min(valid, width - at)) for at in range(0, width, valid)]


def share_start(k, shares, width):
    return pl.multiple_of(lax.rem(lax.axis_index("exp") + k, shares) * width, LANES)


def variance_kernel(variance, *parts):
    shares, width = len(parts), parts[0].shape[2]
    for k in range(shares):
        parts[k][...] = variance[:, :, pl.ds(share_start(k, shares, width), width)]


def edges_kernel(warped, near, far):
    row_count = warped.shape[1]
    even = lax.rem(lax.axis_index("sky"), 2) == 0
    for e in range(warped.shape[0]):
        image = warped[e].astype(F32)
        head, tail = image[:EDGE], image[row_count - EDGE :]
        near[e] = jnp.where(even, tail, head).astype(BF16)
        far[e] = jnp.where(even, head, tail).astype(BF16)


def pieces(value):
    high = value.astype(BF16).astype(F32)
    rest = value - high
    middle = rest.astype(BF16).astype(F32)
    return high, middle, rest - middle


def row_features(first, size, total_rows):
    u = row_position(first, size, total_rows)
    lane = lax.broadcasted_iota(jnp.int32, u.shape, 1)
    power, group = (lane >> 1) & 3, lane >> 3
    value = jnp.where(power == 0, 1.0, jnp.where(power == 1, u, jnp.where(power == 2, u * u, u * u * u)))
    high, middle, low = pieces(value)
    value = jnp.where((group == 1) | (group == 4), middle, jnp.where(group == 2, low, high))
    value = jnp.where(group < PIECES, value, 0.0)
    odd = (lane & 1) == 1
    return jnp.where(odd, 0.0, value).astype(BF16), jnp.where(odd, value, 0.0).astype(BF16)


def setup_kernel(
    total_rows, taps, coeffs, degrees, footprint, masks,
    inner_band, outer_band, col_band, active, covered, inner_features, outer_features
):
    basis_count, _, tap_count = taps.shape
    exp_count, row_count, _ = covered.shape
    half = tap_count // 2
    inner = inner_band.shape[1]

    both = jnp.concatenate([taps[b].astype(F32) for b in range(basis_count)], axis=0)
    lines = jnp.concatenate([both, jnp.zeros((2 * basis_count, LANES - tap_count), F32)], axis=1).astype(BF16)
    lane = lax.broadcasted_iota(jnp.int32, (LANES, LANES), 1)
    tap = lax.broadcasted_iota(jnp.int32, (LANES, LANES), 0)
    flip = (lane + tap == LANES).astype(F32) + ((lane == 0) & (tap == 0)).astype(F32)
    flipped = jnp.dot(lines, flip.astype(BF16), preferred_element_type=F32)
    lines = lines.astype(F32)

    def circulant(line, size):
        return pltpu.roll(jnp.broadcast_to(line, (size, LANES)), 0, 1, stride=1, stride_axis=0)

    near = pltpu.roll(lines, EDGE - half, 1)
    far = pltpu.roll(lines, LANES - 2 * EDGE - half, 1)
    for b in range(basis_count):
        upper = circulant(near[2 * b : 2 * b + 1], inner)
        lower = circulant(far[2 * b : 2 * b + 1], EDGE)
        inner_band[b] = upper.astype(BF16)
        outer_band[b] = jnp.concatenate([upper[:EDGE], lower], axis=0).astype(BF16)
        col_band[b] = circulant(flipped[2 * b + 1 : 2 * b + 2], LANES).astype(BF16)

    term_count = coeffs.shape[2]
    term = lax.broadcasted_iota(jnp.int32, (1, term_count), 1)
    order = jnp.zeros((1, term_count), F32)
    for index, (p, q) in enumerate(POWERS):
        order = jnp.where(term == index, float(p + q), order)
    wide = jnp.concatenate([degrees[...].astype(F32), jnp.zeros((exp_count, LANES - basis_count), F32)], axis=1)
    by_basis = jnp.concatenate([wide, jnp.zeros((8 - exp_count, LANES), F32)], axis=0).T
    local = lax.broadcasted_iota(jnp.int32, (row_count, LANES), 0)
    total = local + lax.axis_index("sky") * row_count
    for e in range(exp_count):
        own = jnp.concatenate([coeffs[b, e : e + 1, :] for b in range(basis_count)], axis=0)
        kept = jnp.where(order <= by_basis[:basis_count, e : e + 1], own, 0.0)
        kept = jnp.concatenate([kept, jnp.zeros((16 - basis_count, term_count), F32)], axis=0)
        kept = jnp.concatenate([kept, jnp.zeros((16, LANES - term_count), F32)], axis=1)
        place = lax.broadcasted_iota(jnp.int32, kept.shape, 1)
        powers = []
        for p in range(4):
            value = jnp.zeros_like(kept)
            for q in range(4 - p):
                value = jnp.where(place == q, pltpu.roll(kept, (q - TERM[p, q]) % LANES, 1), value)
            powers.append(value)
        for pair in range(active.shape[1]):
            active[e, pair] = jnp.concatenate([value[2 * pair : 2 * pair + 2] for value in powers], axis=0)
        word = jnp.broadcast_to(masks[e : e + 1, 0:1], (row_count, LANES))
        first = jnp.zeros((row_count, LANES), jnp.int32)
        for w in range(1, masks.shape[1]):
            here = local >= w * ROWS_PER_WORD
            word = jnp.where(here, jnp.broadcast_to(masks[e : e + 1, w : w + 1], (row_count, LANES)), word)
            first = jnp.where(here, w * ROWS_PER_WORD, first)
        planes = lax.shift_right_logical(word, 2 * (local - first)) & 3
        low = jnp.broadcast_to(footprint[e : e + 1, 0:1], (row_count, LANES))
        high = jnp.broadcast_to(footprint[e : e + 1, 1:2], (row_count, LANES))
        covered[e] = ((total >= low) & (total < high) & (planes != 3)).astype(F32)
    top = lax.axis_index("sky") * row_count
    for odd, value in enumerate(row_features(top + EDGE, inner, total_rows)):
        inner_features[odd * inner : (odd + 1) * inner] = value
    upper = row_features(top, EDGE, total_rows)
    lower = row_features(top + row_count - EDGE, EDGE, total_rows)
    for odd in range(2):
        outer_features[2 * EDGE * odd : 2 * EDGE * (odd + 1)] = jnp.concatenate([upper[odd], lower[odd]], axis=0)


def windows_of(read, start, width, col_count, parts, half):
    left_at = pl.multiple_of(jnp.maximum(start - LANES, 0), LANES)
    right_at = pl.multiple_of(jnp.minimum(start + width, col_count - LANES), LANES)
    left = jnp.where(start > 0, read(left_at, LANES), 0.0)
    right = jnp.where(start + width < col_count, read(right_at, LANES), 0.0)
    middle = read(start, width)
    blocks = [left] + [middle[:, at : at + LANES] for at in range(0, width, LANES)] + [right]
    blocks = [pltpu.roll(block, half, 1) for block in blocks]
    lane = lax.broadcasted_iota(jnp.int32, left.shape, 1)
    place = jnp.where(lane >= half, lane - half, lane - half + LANES)
    pieces = []
    for at, _ in parts:
        base, offset = divmod(LANES + at - half, LANES)
        pieces.append(jnp.where(place >= offset, blocks[base], blocks[base + 1]))
    return jnp.concatenate(pieces, axis=1).astype(BF16)


def line_polynomials(active, lines, start, parts, col_count):
    exp_count, pair_count, rows, _ = active.shape
    lane = lax.broadcasted_iota(jnp.int32, (rows, LANES), 1)
    for s, (at, _) in enumerate(parts):
        col_at = at + jnp.where(lane >= at % LANES, lane - at % LANES, lane - at % LANES + LANES)
        v = (2.0 * (start + col_at).astype(F32) + 1.0) / col_count - 1.0
        span = slice(s * LANES, (s + 1) * LANES)
        for e in range(exp_count):
            for pair in range(pair_count):
                values = active[e, pair]
                c0, c1, c2, c3 = (jnp.broadcast_to(values[:, q : q + 1], values.shape) for q in range(4))
                high, middle, low = pieces(c0 + v * (c1 + v * (c2 + v * c3)))
                lines[e, pair, 0:16, span] = jnp.concatenate([high, high], axis=0).astype(BF16)
                lines[e, pair, 16:32, span] = jnp.concatenate([high, middle], axis=0).astype(BF16)
                lines[e, pair, 32:48, span] = jnp.concatenate([middle, low], axis=0).astype(BF16)


def weighted_sums(e, parts, lines, features, rows, col_band, size):
    out = []
    for first in range(0, len(parts), GROUP):
        members = range(first, min(first + GROUP, len(parts)))
        span = slice(first * LANES, (members[-1] + 1) * LANES)
        totals = [None] * len(members)
        for b in range(col_band.shape[0]):
            odd = b % 2
            if not odd:
                field = jnp.dot(features[:, : 8 * PIECES], lines[e, b // 2, :, span], preferred_element_type=F32)
            window = jnp.concatenate(
                [rows[e, b * size : (b + 1) * size, s * LANES : (s + 1) * LANES] for s in members], axis=0
            )
            along = jnp.dot(window, col_band[b], preferred_element_type=F32)
            for i in range(len(members)):
                weight = field[odd * size : (odd + 1) * size, i * LANES : (i + 1) * LANES]
                value = weight * along[i * size : (i + 1) * size]
                totals[i] = value if b == 0 else totals[i] + value
        out += totals
    return out


def joined(blocks, parts, width):
    out = []
    for low in range(0, width, LANES):
        lane = low + lax.broadcasted_iota(jnp.int32, blocks[0].shape, 1)
        tile = None
        for block, (at, size) in zip(blocks, parts):
            if at < low + LANES and at + size > low:
                tile = block if tile is None else jnp.where(lane >= at, block, tile)
        out.append(tile)
    return jnp.concatenate(out, axis=1)


def row_position(first, rows, total_rows):
    row_at = first + lax.broadcasted_iota(jnp.int32, (rows, LANES), 0)
    return (2.0 * row_at.astype(F32) + 1.0) / total_rows - 1.0


def first_kernel(
    k, shares, half, warped, active, covered, features, inner_band, col_band, matched, lines, strip, rows
):
    exp_count, row_count, col_count = warped.shape
    basis_count, size, _ = inner_band.shape
    _, inner, width = matched.shape
    parts = segments(width, 2 * half + 1)
    start = share_start(k, shares, width)
    line_polynomials(active, lines, start, parts, col_count)
    band = inner_band[...].reshape(basis_count * size, LANES)
    for e in range(exp_count):

        def read(at, count):
            own = warped[e, :, pl.ds(at, count)].astype(F32)
            return jnp.concatenate([own, jnp.zeros((LANES - row_count, count), F32)], axis=0)

        strip[e] = windows_of(read, start, width, col_count, parts, half)
        rows[e] = jnp.dot(band, strip[e], preferred_element_type=F32).astype(BF16)
    for e in range(exp_count):
        blocks = weighted_sums(e, parts, lines, features, rows, col_band, size)
        counts = jnp.concatenate([covered[e, EDGE : EDGE + inner]] * (width // LANES), axis=1) > 0
        matched[e] = jnp.where(counts, joined(blocks, parts, width)[:inner], jnp.inf).astype(BF16)


def second_kernel(
    k, shares, half, warped, near, far, covered, features, outer_band, col_band, lines, matched, strip, rows
):
    exp_count, row_count, col_count = warped.shape
    basis_count, size, _ = outer_band.shape
    width = matched.shape[2]
    parts = segments(width, 2 * half + 1)
    span = LANES // 2 - EDGE
    sky = lax.axis_index("sky")
    even = lax.rem(sky, 2) == 0
    start = share_start(k, shares, width)
    band = outer_band[...].reshape(basis_count * size, LANES)
    for e in range(exp_count):

        def read(at, count):
            own = warped[e, :, pl.ds(at, count)].astype(F32)
            same = near[e, :, pl.ds(at, count)].astype(F32)
            other = far[e, :, pl.ds(at, count)].astype(F32)
            up, down = jnp.where(even, other, same), jnp.where(even, same, other)
            up = jnp.where(sky > 0, up, 0.0)
            down = jnp.where(sky < lax.axis_size("sky") - 1, down, 0.0)
            return jnp.concatenate([up, own[:span], own[row_count - span :], down], axis=0)

        strip[e] = windows_of(read, start, width, col_count, parts, half)
        rows[e] = jnp.dot(band, strip[e], preferred_element_type=F32).astype(BF16)
    for e in range(exp_count):
        blocks = weighted_sums(e, parts, lines, features, rows, col_band, size)
        counts = jnp.concatenate([covered[e, :EDGE], covered[e, row_count - EDGE :]], axis=0)
        counts = jnp.concatenate([counts] * (width // LANES), axis=1) > 0
        matched[e] = jnp.where(counts, joined(blocks, parts, width), jnp.inf).astype(BF16)


def robust_sum(fields, spreads):
    values, variances, weights = [], [], []
    for value, spread in zip(fields, spreads):
        counts = value < jnp.inf
        spread = jnp.where(counts, spread, jnp.inf)
        values.append(jnp.where(counts, value, 0.0))
        variances.append(spread)
        weights.append(1.0 / spread)
    first = sum(w * x for w, x in zip(weights, values)) / (1.0 + sum(weights))
    robust = [1.0 / (s + (x - first) * (x - first) * (1.0 / 9.0)) for s, x in zip(variances, values)]
    return sum(r * x for r, x in zip(robust, values)) / (1.0 + sum(robust))


def first_coadd_kernel(shares, *refs):
    fields, variances, coadd = refs[:shares], refs[shares : 2 * shares], refs[-1]
    exp_count, size, width = fields[0].shape
    pairs = [(k, e) for k in range(shares) for e in range(exp_count)]
    for at in range(0, width, LANES):
        span = slice(at, at + LANES)
        values = [fields[k][e, :, span].astype(F32) for k, e in pairs]
        spreads = [variances[k][e, :, span].astype(F32)[EDGE : EDGE + size] for k, e in pairs]
        coadd[:, span] = robust_sum(values, spreads)


def second_coadd_kernel(shares, *refs):
    fields, variances, done, coadd = refs[:shares], refs[shares : 2 * shares], refs[-2], refs[-1]
    exp_count, row_count, width = variances[0].shape
    size = done.shape[0]
    pairs = [(k, e) for k in range(shares) for e in range(exp_count)]
    coadd[EDGE : EDGE + size] = done[...]
    for at in range(0, width, LANES):
        span = slice(at, at + LANES)
        values = [fields[k][e, :, span].astype(F32) for k, e in pairs]
        spreads = []
        for k, e in pairs:
            spread = variances[k][e, :, span].astype(F32)
            spreads.append(jnp.concatenate([spread[:EDGE], spread[row_count - EDGE :]], axis=0))
        result = robust_sum(values, spreads)
        coadd[:EDGE, span] = result[:EDGE]
        coadd[row_count - EDGE :, span] = result[EDGE:]


def body(warped, variance, basis_taps, coeffs, degrees, footprint, masks):
    exp_count, row_count, col_count = warped.shape
    basis_count, _, tap_count = basis_taps.shape
    half = tap_count // 2
    sky_count, shares = lax.axis_size("sky"), lax.axis_size("exp")
    width = col_count // shares
    total_rows = row_count * sky_count
    inner = row_count - 2 * EDGE
    size = round_up(inner, 16)
    pair_count = -(-basis_count // 2)
    spans = len(segments(width, tap_count)) * LANES
    vmem = pl.BlockSpec(memory_space=pltpu.VMEM)

    def array(*shape, dtype=BF16):
        return jax.ShapeDtypeStruct(shape, dtype)

    def call(kernel, name, out_shape, *operands, scratch=(), mebibytes=8, cost=0.01):
        outputs = len(out_shape) if isinstance(out_shape, list) else 0
        return pl.pallas_call(
            kernel,
            out_shape=out_shape,
            in_specs=[vmem] * len(operands),
            out_specs=[vmem] * outputs if outputs else vmem,
            scratch_shapes=scratch,
            compiler_params=pltpu.CompilerParams(vmem_limit_bytes=mebibytes * 2**20),
            cost_estimate=pl.CostEstimate(flops=int(cost * 1e9), bytes_accessed=int(cost * 3e6), transcendentals=0),
            name=name,
        )(*operands)

    def to_share(values, k):
        return lax.ppermute(values, "exp", [(i, (i + k) % shares) for i in range(shares)])

    variances = call(variance_kernel, "variance", [array(exp_count, row_count, width)] * shares, variance)
    variances = [variances[0]] + [to_share(variances[k], k) for k in range(1, shares)]

    edge = array(exp_count, EDGE, col_count)
    near, far = call(edges_kernel, "edges", [edge, edge], warped)
    near = lax.ppermute(near, "sky", [(i, i ^ 1) for i in range(sky_count) if i ^ 1 < sky_count])
    partner = {i: i + 1 if i % 2 else i - 1 for i in range(1, sky_count)}
    pairs = []
    for i in range(sky_count):
        j = partner.get(i, i)
        ends = j in (i, sky_count)
        for e in range(shares):
            pairs.append((i * shares + e, i * shares + (e + 1) % shares if ends else j * shares + e))
    far = lax.ppermute(far, ("sky", "exp"), pairs)

    inner_band, outer_band, col_band, active, covered, inner_features, outer_features = call(
        functools.partial(setup_kernel, total_rows),
        "setup",
        [
            array(basis_count, size, LANES),
            array(basis_count, 2 * EDGE, LANES),
            array(basis_count, LANES, LANES),
            array(exp_count, pair_count, 8, LANES, dtype=F32),
            array(exp_count, row_count, LANES, dtype=F32),
            array(2 * size, LANES),
            array(4 * EDGE, LANES),
        ],
        basis_taps,
        jnp.transpose(coeffs, (1, 0, 2)),
        degrees,
        footprint,
        masks,
        cost=0.5,
    )

    def first(k):
        return call(
            functools.partial(first_kernel, k, shares, half),
            "first",
            [array(exp_count, inner, width), array(exp_count, pair_count, 8 * PIECES, spans)],
            warped,
            active,
            covered,
            inner_features,
            inner_band,
            col_band,
            scratch=[
                pltpu.VMEM((exp_count, LANES, spans), BF16),
                pltpu.VMEM((exp_count, basis_count * size, spans), BF16),
            ],
            mebibytes=12,
            cost=0.01 if k else 1.5,
        )

    def second(k, near, far, lines):
        return call(
            functools.partial(second_kernel, k, shares, half),
            "second",
            array(exp_count, 2 * EDGE, width),
            warped,
            near,
            far,
            covered,
            outer_features,
            outer_band,
            col_band,
            lines,
            scratch=[
                pltpu.VMEM((exp_count, LANES, spans), BF16),
                pltpu.VMEM((exp_count, basis_count * 2 * EDGE, spans), BF16),
            ],
            mebibytes=12,
            cost=0.01,
        )

    inner_features, near = lax.optimization_barrier((inner_features, near))
    firsts, seconds = [None] * shares, [None] * shares
    held = [None] * shares
    for k in range(1, shares):
        firsts[k], held[k] = first(k)
        firsts[k] = to_share(firsts[k], k)
    firsts[0], held[0] = first(0)
    variances, near, firsts[0] = lax.optimization_barrier((variances, near, firsts[0]))
    for k in range(1, shares):
        seconds[k] = second(k, near, far, held[k])
    seconds[1:], held[0] = lax.optimization_barrier((seconds[1:], held[0]))
    seconds[1:] = [to_share(seconds[k], k) for k in range(1, shares)]
    seconds[0] = second(0, near, far, held[0])

    done = call(
        functools.partial(first_coadd_kernel, shares),
        "first_coadd",
        array(inner, width, dtype=F32),
        *firsts,
        *variances,
        cost=0.01,
    )
    return call(
        functools.partial(second_coadd_kernel, shares),
        "second_coadd",
        array(row_count, width, dtype=F32),
        *seconds,
        *variances,
        done,
        cost=0.01,
    )


def solution(mesh):
    in_specs = (
        P("exp", "sky", None),
        P("exp", "sky", None),
        P(),
        P("exp", None, None),
        P("exp", None),
        P("exp", None),
        P("exp", "sky"),
    )
    return jax.shard_map(body, mesh=mesh, in_specs=in_specs, out_specs=P("sky", "exp"), check_vma=False)
```

```python
import functools

import jax
import jax.numpy as jnp
from jax import lax
from jax.experimental import pallas as pl
from jax.experimental.pallas import tpu as pltpu
from jax.sharding import PartitionSpec as P

POWERS = ((0, 0), (1, 0), (0, 1), (2, 0), (1, 1), (0, 2), (3, 0), (2, 1), (1, 2), (0, 3))
TERM = {power: index for index, power in enumerate(POWERS)}
ROWS_PER_WORD = 15
EDGE = 16
SENT = 12
LANES = 128
GROUP = 3
PIECES = 6
F32 = jnp.float32
BF16 = jnp.bfloat16


def round_up(value, unit):
    return -(-value // unit) * unit


def segments(width, tap_count):
    valid = LANES - tap_count + 1
    return [(at, min(valid, width - at)) for at in range(0, width, valid)]


def share_start(k, shares, width):
    return pl.multiple_of(lax.rem(lax.axis_index("exp") + k, shares) * width, LANES)


def variance_kernel(variance, *parts):
    shares, width = len(parts), parts[0].shape[2]
    for k in range(shares):
        parts[k][...] = variance[:, :, pl.ds(share_start(k, shares, width), width)]


def edges_kernel(warped, near, far):
    exp_count, row_count, _ = warped.shape
    even = lax.rem(lax.axis_index("sky"), 2) == 0
    heads, tails = [], []
    for e in range(exp_count):
        image = warped[e].astype(F32)
        heads.append(image[:SENT])
        tails.append(image[row_count - SENT :])
    head, tail = jnp.concatenate(heads, axis=0), jnp.concatenate(tails, axis=0)
    near[...] = jnp.where(even, tail, head).astype(BF16)
    far[...] = jnp.where(even, head, tail).astype(BF16)


def pieces(value):
    high = value.astype(BF16).astype(F32)
    rest = value - high
    middle = rest.astype(BF16).astype(F32)
    return high, middle, rest - middle


def row_features(first, size, total_rows):
    u = row_position(first, size, total_rows)
    lane = lax.broadcasted_iota(jnp.int32, u.shape, 1)
    power, group = (lane >> 1) & 3, lane >> 3
    value = jnp.where(power == 0, 1.0, jnp.where(power == 1, u, jnp.where(power == 2, u * u, u * u * u)))
    high, middle, low = pieces(value)
    value = jnp.where((group == 1) | (group == 4), middle, jnp.where(group == 2, low, high))
    value = jnp.where(group < PIECES, value, 0.0)
    odd = (lane & 1) == 1
    return jnp.where(odd, 0.0, value).astype(BF16), jnp.where(odd, value, 0.0).astype(BF16)


def setup_kernel(
    total_rows, taps, coeffs, degrees, footprint, masks,
    inner_band, outer_band, col_band, active, covered, inner_features, outer_features
):
    basis_count, _, tap_count = taps.shape
    exp_count, row_count, _ = covered.shape
    half = tap_count // 2
    inner = inner_band.shape[1]

    both = jnp.concatenate([taps[b].astype(F32) for b in range(basis_count)], axis=0)
    lines = jnp.concatenate([both, jnp.zeros((2 * basis_count, LANES - tap_count), F32)], axis=1).astype(BF16)
    lane = lax.broadcasted_iota(jnp.int32, (LANES, LANES), 1)
    tap = lax.broadcasted_iota(jnp.int32, (LANES, LANES), 0)
    flip = (lane + tap == LANES).astype(F32) + ((lane == 0) & (tap == 0)).astype(F32)
    flipped = jnp.dot(lines, flip.astype(BF16), preferred_element_type=F32)
    lines = lines.astype(F32)

    def circulant(line, size):
        return pltpu.roll(jnp.broadcast_to(line, (size, LANES)), 0, 1, stride=1, stride_axis=0)

    near = pltpu.roll(lines, EDGE - half, 1)
    far = pltpu.roll(lines, LANES - 2 * EDGE - half, 1)
    for b in range(basis_count):
        upper = circulant(near[2 * b : 2 * b + 1], inner)
        lower = circulant(far[2 * b : 2 * b + 1], EDGE)
        inner_band[b] = upper.astype(BF16)
        outer_band[b] = jnp.concatenate([upper[:EDGE], lower], axis=0).astype(BF16)
        col_band[b] = circulant(flipped[2 * b + 1 : 2 * b + 2], LANES).astype(BF16)

    term_count = coeffs.shape[2]
    term = lax.broadcasted_iota(jnp.int32, (1, term_count), 1)
    order = jnp.zeros((1, term_count), F32)
    for index, (p, q) in enumerate(POWERS):
        order = jnp.where(term == index, float(p + q), order)
    wide = jnp.concatenate([degrees[...].astype(F32), jnp.zeros((exp_count, LANES - basis_count), F32)], axis=1)
    by_basis = jnp.concatenate([wide, jnp.zeros((8 - exp_count, LANES), F32)], axis=0).T
    local = lax.broadcasted_iota(jnp.int32, (row_count, LANES), 0)
    total = local + lax.axis_index("sky") * row_count
    for e in range(exp_count):
        own = jnp.concatenate([coeffs[b, e : e + 1, :] for b in range(basis_count)], axis=0)
        kept = jnp.where(order <= by_basis[:basis_count, e : e + 1], own, 0.0)
        kept = jnp.concatenate([kept, jnp.zeros((16 - basis_count, term_count), F32)], axis=0)
        kept = jnp.concatenate([kept, jnp.zeros((16, LANES - term_count), F32)], axis=1)
        place = lax.broadcasted_iota(jnp.int32, kept.shape, 1)
        powers = []
        for p in range(4):
            value = jnp.zeros_like(kept)
            for q in range(4 - p):
                value = jnp.where(place == q, pltpu.roll(kept, (q - TERM[p, q]) % LANES, 1), value)
            powers.append(value)
        for pair in range(active.shape[1]):
            active[e, pair] = jnp.concatenate([value[2 * pair : 2 * pair + 2] for value in powers], axis=0)
        word = jnp.broadcast_to(masks[e : e + 1, 0:1], (row_count, LANES))
        first = jnp.zeros((row_count, LANES), jnp.int32)
        for w in range(1, masks.shape[1]):
            here = local >= w * ROWS_PER_WORD
            word = jnp.where(here, jnp.broadcast_to(masks[e : e + 1, w : w + 1], (row_count, LANES)), word)
            first = jnp.where(here, w * ROWS_PER_WORD, first)
        planes = lax.shift_right_logical(word, 2 * (local - first)) & 3
        low = jnp.broadcast_to(footprint[e : e + 1, 0:1], (row_count, LANES))
        high = jnp.broadcast_to(footprint[e : e + 1, 1:2], (row_count, LANES))
        covered[e] = ((total >= low) & (total < high) & (planes != 3)).astype(F32)
    top = lax.axis_index("sky") * row_count
    for odd, value in enumerate(row_features(top + EDGE, inner, total_rows)):
        inner_features[odd * inner : (odd + 1) * inner] = value
    upper = row_features(top, EDGE, total_rows)
    lower = row_features(top + row_count - EDGE, EDGE, total_rows)
    for odd in range(2):
        outer_features[2 * EDGE * odd : 2 * EDGE * (odd + 1)] = jnp.concatenate([upper[odd], lower[odd]], axis=0)


def windows_of(read, start, width, col_count, parts, half):
    left_at = pl.multiple_of(jnp.maximum(start - LANES, 0), LANES)
    right_at = pl.multiple_of(jnp.minimum(start + width, col_count - LANES), LANES)
    left = jnp.where(start > 0, read(left_at, LANES), 0.0)
    right = jnp.where(start + width < col_count, read(right_at, LANES), 0.0)
    middle = read(start, width)
    blocks = [left] + [middle[:, at : at + LANES] for at in range(0, width, LANES)] + [right]
    blocks = [pltpu.roll(block, half, 1) for block in blocks]
    lane = lax.broadcasted_iota(jnp.int32, left.shape, 1)
    place = jnp.where(lane >= half, lane - half, lane - half + LANES)
    pieces = []
    for at, _ in parts:
        base, offset = divmod(LANES + at - half, LANES)
        pieces.append(jnp.where(place >= offset, blocks[base], blocks[base + 1]))
    return jnp.concatenate(pieces, axis=1).astype(BF16)


def line_polynomials(active, lines, start, parts, col_count):
    exp_count, pair_count, rows, _ = active.shape
    lane = lax.broadcasted_iota(jnp.int32, (rows, LANES), 1)
    for s, (at, _) in enumerate(parts):
        col_at = at + jnp.where(lane >= at % LANES, lane - at % LANES, lane - at % LANES + LANES)
        v = (2.0 * (start + col_at).astype(F32) + 1.0) / col_count - 1.0
        span = slice(s * LANES, (s + 1) * LANES)
        for e in range(exp_count):
            for pair in range(pair_count):
                values = active[e, pair]
                c0, c1, c2, c3 = (jnp.broadcast_to(values[:, q : q + 1], values.shape) for q in range(4))
                high, middle, low = pieces(c0 + v * (c1 + v * (c2 + v * c3)))
                lines[e, pair, 0:16, span] = jnp.concatenate([high, high], axis=0).astype(BF16)
                lines[e, pair, 16:32, span] = jnp.concatenate([high, middle], axis=0).astype(BF16)
                lines[e, pair, 32:48, span] = jnp.concatenate([middle, low], axis=0).astype(BF16)


def weighted_sums(e, parts, lines, features, rows, col_band, size):
    out = []
    for first in range(0, len(parts), GROUP):
        members = range(first, min(first + GROUP, len(parts)))
        span = slice(first * LANES, (members[-1] + 1) * LANES)
        totals = [None] * len(members)
        for b in range(col_band.shape[0]):
            odd = b % 2
            if not odd:
                field = jnp.dot(features[:, : 8 * PIECES], lines[e, b // 2, :, span], preferred_element_type=F32)
            window = jnp.concatenate(
                [rows[e, b * size : (b + 1) * size, s * LANES : (s + 1) * LANES] for s in members], axis=0
            )
            along = jnp.dot(window, col_band[b], preferred_element_type=F32)
            for i in range(len(members)):
                weight = field[odd * size : (odd + 1) * size, i * LANES : (i + 1) * LANES]
                value = weight * along[i * size : (i + 1) * size]
                totals[i] = value if b == 0 else totals[i] + value
        out += totals
    return out


def joined(blocks, parts, width):
    out = []
    for low in range(0, width, LANES):
        lane = low + lax.broadcasted_iota(jnp.int32, blocks[0].shape, 1)
        tile = None
        for block, (at, size) in zip(blocks, parts):
            if at < low + LANES and at + size > low:
                tile = block if tile is None else jnp.where(lane >= at, block, tile)
        out.append(tile)
    return jnp.concatenate(out, axis=1)


def row_position(first, rows, total_rows):
    row_at = first + lax.broadcasted_iota(jnp.int32, (rows, LANES), 0)
    return (2.0 * row_at.astype(F32) + 1.0) / total_rows - 1.0


def first_kernel(
    k, shares, half, warped, active, covered, features, inner_band, col_band, matched, lines, strip, rows
):
    exp_count, row_count, col_count = warped.shape
    basis_count, size, _ = inner_band.shape
    _, inner, width = matched.shape
    parts = segments(width, 2 * half + 1)
    start = share_start(k, shares, width)
    line_polynomials(active, lines, start, parts, col_count)
    band = inner_band[...].reshape(basis_count * size, LANES)
    for e in range(exp_count):

        def read(at, count):
            own = warped[e, :, pl.ds(at, count)].astype(F32)
            return jnp.concatenate([own, jnp.zeros((LANES - row_count, count), F32)], axis=0)

        strip[e] = windows_of(read, start, width, col_count, parts, half)
        rows[e] = jnp.dot(band, strip[e], preferred_element_type=F32).astype(BF16)
    for e in range(exp_count):
        blocks = weighted_sums(e, parts, lines, features, rows, col_band, size)
        counts = jnp.concatenate([covered[e, EDGE : EDGE + inner]] * (width // LANES), axis=1) > 0
        matched[e] = jnp.where(counts, joined(blocks, parts, width)[:inner], jnp.inf).astype(BF16)


def second_kernel(
    k, shares, half, warped, near, far, covered, features, outer_band, col_band, lines, matched, strip, rows
):
    exp_count, row_count, col_count = warped.shape
    basis_count, size, _ = outer_band.shape
    width = matched.shape[2]
    parts = segments(width, 2 * half + 1)
    span = LANES // 2 - EDGE
    sky = lax.axis_index("sky")
    even = lax.rem(sky, 2) == 0
    start = share_start(k, shares, width)
    band = outer_band[...].reshape(basis_count * size, LANES)
    for e in range(exp_count):

        def read(at, count):
            own = warped[e, :, pl.ds(at, count)].astype(F32)
            same = near[:, pl.ds(at, count)].astype(F32)[e * SENT : (e + 1) * SENT]
            other = far[:, pl.ds(at, count)].astype(F32)[e * SENT : (e + 1) * SENT]
            up, down = jnp.where(even, other, same), jnp.where(even, same, other)
            up = jnp.where(sky > 0, up, 0.0)
            down = jnp.where(sky < lax.axis_size("sky") - 1, down, 0.0)
            gap = jnp.zeros((EDGE - SENT, count), F32)
            return jnp.concatenate([gap, up, own[:span], own[row_count - span :], down, gap], axis=0)

        strip[e] = windows_of(read, start, width, col_count, parts, half)
        rows[e] = jnp.dot(band, strip[e], preferred_element_type=F32).astype(BF16)
    for e in range(exp_count):
        blocks = weighted_sums(e, parts, lines, features, rows, col_band, size)
        counts = jnp.concatenate([covered[e, :EDGE], covered[e, row_count - EDGE :]], axis=0)
        counts = jnp.concatenate([counts] * (width // LANES), axis=1) > 0
        matched[e] = jnp.where(counts, joined(blocks, parts, width), jnp.inf).astype(BF16)


def robust_sum(fields, spreads):
    values, variances, weights = [], [], []
    for value, spread in zip(fields, spreads):
        counts = value < jnp.inf
        spread = jnp.where(counts, spread, jnp.inf)
        values.append(jnp.where(counts, value, 0.0))
        variances.append(spread)
        weights.append(1.0 / spread)
    first = sum(w * x for w, x in zip(weights, values)) / (1.0 + sum(weights))
    robust = [1.0 / (s + (x - first) * (x - first) * (1.0 / 9.0)) for s, x in zip(variances, values)]
    return sum(r * x for r, x in zip(robust, values)) / (1.0 + sum(robust))


def first_coadd_kernel(shares, *refs):
    fields, variances, coadd = refs[:shares], refs[shares : 2 * shares], refs[-1]
    exp_count, size, width = fields[0].shape
    pairs = [(k, e) for k in range(shares) for e in range(exp_count)]
    for at in range(0, width, LANES):
        span = slice(at, at + LANES)
        values = [fields[k][e, :, span].astype(F32) for k, e in pairs]
        spreads = [variances[k][e, :, span].astype(F32)[EDGE : EDGE + size] for k, e in pairs]
        coadd[:, span] = robust_sum(values, spreads)


def second_coadd_kernel(shares, *refs):
    fields, variances, done = refs[:shares], refs[shares : 2 * shares], refs[2 * shares]
    coadd, edges, copied = refs[2 * shares + 1 :]
    exp_count, row_count, width = variances[0].shape
    size = done.shape[0]
    pairs = [(k, e) for k in range(shares) for e in range(exp_count)]
    inner = pltpu.make_async_copy(done, coadd.at[EDGE : EDGE + size], copied.at[0])
    inner.start()
    for at in range(0, width, LANES):
        span = slice(at, at + LANES)
        values = [fields[k][e, :, span].astype(F32) for k, e in pairs]
        spreads = []
        for k, e in pairs:
            spread = variances[k][e, :, span].astype(F32)
            spreads.append(jnp.concatenate([spread[:EDGE], spread[row_count - EDGE :]], axis=0))
        edges[:, span] = robust_sum(values, spreads)
    upper = pltpu.make_async_copy(edges.at[:EDGE], coadd.at[:EDGE], copied.at[1])
    lower = pltpu.make_async_copy(edges.at[EDGE:], coadd.at[row_count - EDGE :], copied.at[2])
    upper.start()
    lower.start()
    inner.wait()
    upper.wait()
    lower.wait()


def body(warped, variance, basis_taps, coeffs, degrees, footprint, masks):
    exp_count, row_count, col_count = warped.shape
    basis_count, _, tap_count = basis_taps.shape
    half = tap_count // 2
    sky_count, shares = lax.axis_size("sky"), lax.axis_size("exp")
    width = col_count // shares
    total_rows = row_count * sky_count
    inner = row_count - 2 * EDGE
    size = round_up(inner, 16)
    pair_count = -(-basis_count // 2)
    spans = len(segments(width, tap_count)) * LANES
    vmem = pl.BlockSpec(memory_space=pltpu.VMEM)

    def array(*shape, dtype=BF16):
        return jax.ShapeDtypeStruct(shape, dtype)

    def call(kernel, name, out_shape, *operands, scratch=(), mebibytes=8, cost=0.01):
        outputs = len(out_shape) if isinstance(out_shape, list) else 0
        return pl.pallas_call(
            kernel,
            out_shape=out_shape,
            in_specs=[vmem] * len(operands),
            out_specs=[vmem] * outputs if outputs else vmem,
            scratch_shapes=scratch,
            compiler_params=pltpu.CompilerParams(vmem_limit_bytes=mebibytes * 2**20),
            cost_estimate=pl.CostEstimate(flops=int(cost * 1e9), bytes_accessed=int(cost * 3e6), transcendentals=0),
            name=name,
        )(*operands)

    def to_share(values, k):
        return lax.ppermute(values, "exp", [(i, (i + k) % shares) for i in range(shares)])

    variances = call(variance_kernel, "variance", [array(exp_count, row_count, width)] * shares, variance)
    variances = [variances[0]] + [to_share(variances[k], k) for k in range(1, shares)]

    edge = array(exp_count * SENT, col_count)
    near, far = call(edges_kernel, "edges", [edge, edge], warped)
    near = lax.ppermute(near, "sky", [(i, i ^ 1) for i in range(sky_count) if i ^ 1 < sky_count])
    partner = {i: i + 1 if i % 2 else i - 1 for i in range(1, sky_count)}
    pairs = []
    for i in range(sky_count):
        j = partner.get(i, i)
        ends = j in (i, sky_count)
        for e in range(shares):
            pairs.append((i * shares + e, i * shares + (e + 1) % shares if ends else j * shares + e))
    far = lax.ppermute(far, ("sky", "exp"), pairs)

    inner_band, outer_band, col_band, active, covered, inner_features, outer_features = call(
        functools.partial(setup_kernel, total_rows),
        "setup",
        [
            array(basis_count, size, LANES),
            array(basis_count, 2 * EDGE, LANES),
            array(basis_count, LANES, LANES),
            array(exp_count, pair_count, 8, LANES, dtype=F32),
            array(exp_count, row_count, LANES, dtype=F32),
            array(2 * size, LANES),
            array(4 * EDGE, LANES),
        ],
        basis_taps,
        jnp.transpose(coeffs, (1, 0, 2)),
        degrees,
        footprint,
        masks,
        cost=0.5,
    )

    def first(k):
        return call(
            functools.partial(first_kernel, k, shares, half),
            "first",
            [array(exp_count, inner, width), array(exp_count, pair_count, 8 * PIECES, spans)],
            warped,
            active,
            covered,
            inner_features,
            inner_band,
            col_band,
            scratch=[
                pltpu.VMEM((exp_count, LANES, spans), BF16),
                pltpu.VMEM((exp_count, basis_count * size, spans), BF16),
            ],
            mebibytes=12,
            cost=0.01 if k else 1.5,
        )

    def second(k, near, far, lines):
        return call(
            functools.partial(second_kernel, k, shares, half),
            "second",
            array(exp_count, 2 * EDGE, width),
            warped,
            near,
            far,
            covered,
            outer_features,
            outer_band,
            col_band,
            lines,
            scratch=[
                pltpu.VMEM((exp_count, LANES, spans), BF16),
                pltpu.VMEM((exp_count, basis_count * 2 * EDGE, spans), BF16),
            ],
            mebibytes=12,
            cost=0.01,
        )

    inner_features, near = lax.optimization_barrier((inner_features, near))
    firsts, seconds = [None] * shares, [None] * shares
    held = [None] * shares
    for k in range(1, shares):
        firsts[k], held[k] = first(k)
        firsts[k] = to_share(firsts[k], k)
    firsts[0], held[0] = first(0)
    variances, near, firsts[0] = lax.optimization_barrier((variances, near, firsts[0]))
    for k in range(1, shares):
        seconds[k] = second(k, near, far, held[k])
    seconds[1:], held[0] = lax.optimization_barrier((seconds[1:], held[0]))
    seconds[1:] = [to_share(seconds[k], k) for k in range(1, shares)]
    seconds[0] = second(0, near, far, held[0])

    done = call(
        functools.partial(first_coadd_kernel, shares),
        "first_coadd",
        array(inner, width, dtype=F32),
        *firsts,
        *variances,
        cost=0.01,
    )
    return pl.pallas_call(
        functools.partial(second_coadd_kernel, shares),
        out_shape=array(row_count, width, dtype=F32),
        in_specs=[vmem] * (2 * shares + 1),
        out_specs=pl.BlockSpec(memory_space=pl.ANY),
        scratch_shapes=[pltpu.VMEM((2 * EDGE, width), F32), pltpu.SemaphoreType.DMA((3,))],
        compiler_params=pltpu.CompilerParams(vmem_limit_bytes=8 * 2**20),
        name="second_coadd",
    )(*seconds, *variances, done)


def solution(mesh):
    in_specs = (
        P("exp", "sky", None),
        P("exp", "sky", None),
        P(),
        P("exp", None, None),
        P("exp", None),
        P("exp", None),
        P("exp", "sky"),
    )
    return jax.shard_map(body, mesh=mesh, in_specs=in_specs, out_specs=P("sky", "exp"), check_vma=False)
```

```python
import functools

import jax
import jax.numpy as jnp
from jax import lax
from jax.experimental import pallas as pl
from jax.experimental.pallas import tpu as pltpu
from jax.sharding import PartitionSpec as P

POWERS = ((0, 0), (1, 0), (0, 1), (2, 0), (1, 1), (0, 2), (3, 0), (2, 1), (1, 2), (0, 3))
TERM = {power: index for index, power in enumerate(POWERS)}
ROWS_PER_WORD = 15
EDGE = 16
SENT = 12
LANES = 128
GROUP = 3
PIECES = 6
F32 = jnp.float32
BF16 = jnp.bfloat16


def round_up(value, unit):
    return -(-value // unit) * unit


def segments(width, tap_count):
    valid = LANES - tap_count + 1
    return [(at, min(valid, width - at)) for at in range(0, width, valid)]


def share_start(k, shares, width):
    return pl.multiple_of(lax.rem(lax.axis_index("exp") + k, shares) * width, LANES)


def variance_kernel(variance, *parts):
    shares, width = len(parts), parts[0].shape[2]
    for k in range(shares):
        parts[k][...] = variance[:, :, pl.ds(share_start(k, shares, width), width)]


def edges_kernel(warped, near, far):
    exp_count, row_count, _ = warped.shape
    even = lax.rem(lax.axis_index("sky"), 2) == 0
    heads, tails = [], []
    for e in range(exp_count):
        image = warped[e].astype(F32)
        heads.append(image[:SENT])
        tails.append(image[row_count - SENT :])
    head, tail = jnp.concatenate(heads, axis=0), jnp.concatenate(tails, axis=0)
    near[...] = jnp.where(even, tail, head).astype(BF16)
    far[...] = jnp.where(even, head, tail).astype(BF16)


def pieces(value):
    high = value.astype(BF16).astype(F32)
    rest = value - high
    middle = rest.astype(BF16).astype(F32)
    return high, middle, rest - middle


def row_features(first, size, total_rows):
    u = row_position(first, size, total_rows)
    lane = lax.broadcasted_iota(jnp.int32, u.shape, 1)
    power, group = (lane >> 1) & 3, lane >> 3
    value = jnp.where(power == 0, 1.0, jnp.where(power == 1, u, jnp.where(power == 2, u * u, u * u * u)))
    high, middle, low = pieces(value)
    value = jnp.where((group == 1) | (group == 4), middle, jnp.where(group == 2, low, high))
    value = jnp.where(group < PIECES, value, 0.0)
    odd = (lane & 1) == 1
    return jnp.where(odd, 0.0, value).astype(BF16), jnp.where(odd, value, 0.0).astype(BF16)


def setup_kernel(
    total_rows, taps, coeffs, degrees, footprint, masks,
    inner_band, outer_band, col_band, active, covered, inner_features, outer_features
):
    basis_count, _, tap_count = taps.shape
    exp_count, row_count, _ = covered.shape
    half = tap_count // 2
    inner = inner_band.shape[1]

    both = jnp.concatenate([taps[b].astype(F32) for b in range(basis_count)], axis=0)
    lines = jnp.concatenate([both, jnp.zeros((2 * basis_count, LANES - tap_count), F32)], axis=1).astype(BF16)
    lane = lax.broadcasted_iota(jnp.int32, (LANES, LANES), 1)
    tap = lax.broadcasted_iota(jnp.int32, (LANES, LANES), 0)
    flip = (lane + tap == LANES).astype(F32) + ((lane == 0) & (tap == 0)).astype(F32)
    flipped = jnp.dot(lines, flip.astype(BF16), preferred_element_type=F32)
    lines = lines.astype(F32)

    def circulant(line, size):
        return pltpu.roll(jnp.broadcast_to(line, (size, LANES)), 0, 1, stride=1, stride_axis=0)

    near = pltpu.roll(lines, EDGE - half, 1)
    far = pltpu.roll(lines, LANES - 2 * EDGE - half, 1)
    for b in range(basis_count):
        upper = circulant(near[2 * b : 2 * b + 1], inner)
        lower = circulant(far[2 * b : 2 * b + 1], EDGE)
        inner_band[b] = upper.astype(BF16)
        outer_band[b] = jnp.concatenate([upper[:EDGE], lower], axis=0).astype(BF16)
        col_band[b] = circulant(flipped[2 * b + 1 : 2 * b + 2], LANES).astype(BF16)

    term_count = coeffs.shape[2]
    term = lax.broadcasted_iota(jnp.int32, (1, term_count), 1)
    order = jnp.zeros((1, term_count), F32)
    for index, (p, q) in enumerate(POWERS):
        order = jnp.where(term == index, float(p + q), order)
    wide = jnp.concatenate([degrees[...].astype(F32), jnp.zeros((exp_count, LANES - basis_count), F32)], axis=1)
    by_basis = jnp.concatenate([wide, jnp.zeros((8 - exp_count, LANES), F32)], axis=0).T
    local = lax.broadcasted_iota(jnp.int32, (row_count, LANES), 0)
    total = local + lax.axis_index("sky") * row_count
    for e in range(exp_count):
        own = jnp.concatenate([coeffs[b, e : e + 1, :] for b in range(basis_count)], axis=0)
        kept = jnp.where(order <= by_basis[:basis_count, e : e + 1], own, 0.0)
        kept = jnp.concatenate([kept, jnp.zeros((16 - basis_count, term_count), F32)], axis=0)
        kept = jnp.concatenate([kept, jnp.zeros((16, LANES - term_count), F32)], axis=1)
        place = lax.broadcasted_iota(jnp.int32, kept.shape, 1)
        powers = []
        for p in range(4):
            value = jnp.zeros_like(kept)
            for q in range(4 - p):
                value = jnp.where(place == q, pltpu.roll(kept, (q - TERM[p, q]) % LANES, 1), value)
            powers.append(value)
        for pair in range(active.shape[1]):
            active[e, pair] = jnp.concatenate([value[2 * pair : 2 * pair + 2] for value in powers], axis=0)
        word = jnp.broadcast_to(masks[e : e + 1, 0:1], (row_count, LANES))
        first = jnp.zeros((row_count, LANES), jnp.int32)
        for w in range(1, masks.shape[1]):
            here = local >= w * ROWS_PER_WORD
            word = jnp.where(here, jnp.broadcast_to(masks[e : e + 1, w : w + 1], (row_count, LANES)), word)
            first = jnp.where(here, w * ROWS_PER_WORD, first)
        planes = lax.shift_right_logical(word, 2 * (local - first)) & 3
        low = jnp.broadcast_to(footprint[e : e + 1, 0:1], (row_count, LANES))
        high = jnp.broadcast_to(footprint[e : e + 1, 1:2], (row_count, LANES))
        covered[e] = ((total >= low) & (total < high) & (planes != 3)).astype(F32)
    top = lax.axis_index("sky") * row_count
    for odd, value in enumerate(row_features(top + EDGE, inner, total_rows)):
        inner_features[odd * inner : (odd + 1) * inner] = value
    upper = row_features(top, EDGE, total_rows)
    lower = row_features(top + row_count - EDGE, EDGE, total_rows)
    for odd in range(2):
        outer_features[2 * EDGE * odd : 2 * EDGE * (odd + 1)] = jnp.concatenate([upper[odd], lower[odd]], axis=0)


def windows_of(read, start, width, col_count, parts, half):
    left_at = pl.multiple_of(jnp.maximum(start - LANES, 0), LANES)
    right_at = pl.multiple_of(jnp.minimum(start + width, col_count - LANES), LANES)
    left = jnp.where(start > 0, read(left_at, LANES), 0.0)
    right = jnp.where(start + width < col_count, read(right_at, LANES), 0.0)
    middle = read(start, width)
    blocks = [left] + [middle[:, at : at + LANES] for at in range(0, width, LANES)] + [right]
    blocks = [pltpu.roll(block, half, 1) for block in blocks]
    lane = lax.broadcasted_iota(jnp.int32, left.shape, 1)
    place = jnp.where(lane >= half, lane - half, lane - half + LANES)
    pieces = []
    for at, _ in parts:
        base, offset = divmod(LANES + at - half, LANES)
        pieces.append(jnp.where(place >= offset, blocks[base], blocks[base + 1]))
    return jnp.concatenate(pieces, axis=1).astype(BF16)


def line_polynomials(active, lines, start, parts, col_count):
    exp_count, pair_count, rows, _ = active.shape
    lane = lax.broadcasted_iota(jnp.int32, (rows, LANES), 1)
    for s, (at, _) in enumerate(parts):
        col_at = at + jnp.where(lane >= at % LANES, lane - at % LANES, lane - at % LANES + LANES)
        v = (2.0 * (start + col_at).astype(F32) + 1.0) / col_count - 1.0
        span = slice(s * LANES, (s + 1) * LANES)
        for e in range(exp_count):
            for pair in range(pair_count):
                values = active[e, pair]
                c0, c1, c2, c3 = (jnp.broadcast_to(values[:, q : q + 1], values.shape) for q in range(4))
                high, middle, low = pieces(c0 + v * (c1 + v * (c2 + v * c3)))
                lines[e, pair, 0:16, span] = jnp.concatenate([high, high], axis=0).astype(BF16)
                lines[e, pair, 16:32, span] = jnp.concatenate([high, middle], axis=0).astype(BF16)
                lines[e, pair, 32:48, span] = jnp.concatenate([middle, low], axis=0).astype(BF16)


def weighted_sums(members, lines, features, rows, col_band, size):
    spans = [slice(s * LANES, (s + 1) * LANES) for _, s in members]
    exposures = sorted({e for e, _ in members})
    totals = [None] * len(members)
    for b in range(col_band.shape[0]):
        odd = b % 2
        if not odd:
            fields = {}
            for e in exposures:
                own = [s for other, s in members if other == e]
                columns = lines[e, b // 2, :, own[0] * LANES : (own[-1] + 1) * LANES]
                product = jnp.dot(features[:, : 8 * PIECES], columns, preferred_element_type=F32)
                for i, s in enumerate(own):
                    fields[e, s] = product[:, i * LANES : (i + 1) * LANES]
        window = jnp.concatenate(
            [rows[e, b * size : (b + 1) * size, span] for (e, _), span in zip(members, spans)], axis=0
        )
        along = jnp.dot(window, col_band[b], preferred_element_type=F32)
        for i, member in enumerate(members):
            value = fields[member][odd * size : (odd + 1) * size] * along[i * size : (i + 1) * size]
            totals[i] = value if b == 0 else totals[i] + value
    return totals


def joined(blocks, parts, width):
    out = []
    for low in range(0, width, LANES):
        lane = low + lax.broadcasted_iota(jnp.int32, blocks[0].shape, 1)
        tile = None
        for block, (at, size) in zip(blocks, parts):
            if at < low + LANES and at + size > low:
                tile = block if tile is None else jnp.where(lane >= at, block, tile)
        out.append(tile)
    return jnp.concatenate(out, axis=1)


def row_position(first, rows, total_rows):
    row_at = first + lax.broadcasted_iota(jnp.int32, (rows, LANES), 0)
    return (2.0 * row_at.astype(F32) + 1.0) / total_rows - 1.0


def first_kernel(
    k, shares, half, warped, active, covered, features, inner_band, col_band, matched, lines, strip, rows
):
    exp_count, row_count, col_count = warped.shape
    basis_count, size, _ = inner_band.shape
    _, inner, width = matched.shape
    parts = segments(width, 2 * half + 1)
    start = share_start(k, shares, width)
    line_polynomials(active, lines, start, parts, col_count)
    band = inner_band[...].reshape(basis_count * size, LANES)
    for e in range(exp_count):

        def read(at, count):
            own = warped[e, :, pl.ds(at, count)].astype(F32)
            return jnp.concatenate([own, jnp.zeros((LANES - row_count, count), F32)], axis=0)

        strip[e] = windows_of(read, start, width, col_count, parts, half)
        rows[e] = jnp.dot(band, strip[e], preferred_element_type=F32).astype(BF16)
    for e in range(exp_count):
        blocks = []
        for low in range(0, len(parts), GROUP):
            members = [(e, s) for s in range(low, min(low + GROUP, len(parts)))]
            blocks += weighted_sums(members, lines, features, rows, col_band, size)
        counts = jnp.concatenate([covered[e, EDGE : EDGE + inner]] * (width // LANES), axis=1) > 0
        matched[e] = jnp.where(counts, joined(blocks, parts, width)[:inner], jnp.inf).astype(BF16)


def second_kernel(
    k, shares, half, warped, near, far, covered, features, outer_band, col_band, lines, matched, strip, rows
):
    exp_count, row_count, col_count = warped.shape
    basis_count, size, _ = outer_band.shape
    width = matched.shape[2]
    parts = segments(width, 2 * half + 1)
    span = LANES // 2 - EDGE
    sky = lax.axis_index("sky")
    even = lax.rem(sky, 2) == 0
    start = share_start(k, shares, width)
    band = outer_band[...].reshape(basis_count * size, LANES)
    for e in range(exp_count):

        def read(at, count):
            own = warped[e, :, pl.ds(at, count)].astype(F32)
            same = near[:, pl.ds(at, count)].astype(F32)[e * SENT : (e + 1) * SENT]
            other = far[:, pl.ds(at, count)].astype(F32)[e * SENT : (e + 1) * SENT]
            up, down = jnp.where(even, other, same), jnp.where(even, same, other)
            up = jnp.where(sky > 0, up, 0.0)
            down = jnp.where(sky < lax.axis_size("sky") - 1, down, 0.0)
            gap = jnp.zeros((EDGE - SENT, count), F32)
            return jnp.concatenate([gap, up, own[:span], own[row_count - span :], down, gap], axis=0)

        strip[e] = windows_of(read, start, width, col_count, parts, half)
        rows[e] = jnp.dot(band, strip[e], preferred_element_type=F32).astype(BF16)
    members = [(e, s) for e in range(exp_count) for s in range(len(parts))]
    every = weighted_sums(members, lines, features, rows, col_band, size)
    for e in range(exp_count):
        blocks = every[e * len(parts) : (e + 1) * len(parts)]
        counts = jnp.concatenate([covered[e, :EDGE], covered[e, row_count - EDGE :]], axis=0)
        counts = jnp.concatenate([counts] * (width // LANES), axis=1) > 0
        matched[e] = jnp.where(counts, joined(blocks, parts, width), jnp.inf).astype(BF16)


def robust_sum(fields, spreads):
    values, variances, weights = [], [], []
    for value, spread in zip(fields, spreads):
        counts = value < jnp.inf
        spread = jnp.where(counts, spread, jnp.inf)
        values.append(jnp.where(counts, value, 0.0))
        variances.append(spread)
        weights.append(1.0 / spread)
    first = sum(w * x for w, x in zip(weights, values)) / (1.0 + sum(weights))
    robust = [1.0 / (s + (x - first) * (x - first) * (1.0 / 9.0)) for s, x in zip(variances, values)]
    return sum(r * x for r, x in zip(robust, values)) / (1.0 + sum(robust))


def first_coadd_kernel(shares, *refs):
    fields, variances, coadd = refs[:shares], refs[shares : 2 * shares], refs[-1]
    exp_count, size, width = fields[0].shape
    pairs = [(k, e) for k in range(shares) for e in range(exp_count)]
    for at in range(0, width, LANES):
        span = slice(at, at + LANES)
        values = [fields[k][e, :, span].astype(F32) for k, e in pairs]
        spreads = [variances[k][e, :, span].astype(F32)[EDGE : EDGE + size] for k, e in pairs]
        coadd[:, span] = robust_sum(values, spreads)


def second_coadd_kernel(shares, *refs):
    fields, variances, done = refs[:shares], refs[shares : 2 * shares], refs[2 * shares]
    coadd, edges, copied = refs[2 * shares + 1 :]
    exp_count, row_count, width = variances[0].shape
    size = done.shape[0]
    pairs = [(k, e) for k in range(shares) for e in range(exp_count)]
    inner = pltpu.make_async_copy(done, coadd.at[EDGE : EDGE + size], copied.at[0])
    inner.start()
    for at in range(0, width, LANES):
        span = slice(at, at + LANES)
        values = [fields[k][e, :, span].astype(F32) for k, e in pairs]
        spreads = []
        for k, e in pairs:
            spread = variances[k][e, :, span].astype(F32)
            spreads.append(jnp.concatenate([spread[:EDGE], spread[row_count - EDGE :]], axis=0))
        edges[:, span] = robust_sum(values, spreads)
    upper = pltpu.make_async_copy(edges.at[:EDGE], coadd.at[:EDGE], copied.at[1])
    lower = pltpu.make_async_copy(edges.at[EDGE:], coadd.at[row_count - EDGE :], copied.at[2])
    upper.start()
    lower.start()
    inner.wait()
    upper.wait()
    lower.wait()


def body(warped, variance, basis_taps, coeffs, degrees, footprint, masks):
    exp_count, row_count, col_count = warped.shape
    basis_count, _, tap_count = basis_taps.shape
    half = tap_count // 2
    sky_count, shares = lax.axis_size("sky"), lax.axis_size("exp")
    width = col_count // shares
    total_rows = row_count * sky_count
    inner = row_count - 2 * EDGE
    size = round_up(inner, 16)
    pair_count = -(-basis_count // 2)
    spans = len(segments(width, tap_count)) * LANES
    vmem = pl.BlockSpec(memory_space=pltpu.VMEM)

    def array(*shape, dtype=BF16):
        return jax.ShapeDtypeStruct(shape, dtype)

    def call(kernel, name, out_shape, *operands, scratch=(), mebibytes=8, cost=0.01):
        outputs = len(out_shape) if isinstance(out_shape, list) else 0
        return pl.pallas_call(
            kernel,
            out_shape=out_shape,
            in_specs=[vmem] * len(operands),
            out_specs=[vmem] * outputs if outputs else vmem,
            scratch_shapes=scratch,
            compiler_params=pltpu.CompilerParams(vmem_limit_bytes=mebibytes * 2**20),
            cost_estimate=pl.CostEstimate(flops=int(cost * 1e9), bytes_accessed=int(cost * 3e6), transcendentals=0),
            name=name,
        )(*operands)

    def to_share(values, k):
        return lax.ppermute(values, "exp", [(i, (i + k) % shares) for i in range(shares)])

    variances = call(variance_kernel, "variance", [array(exp_count, row_count, width)] * shares, variance)
    variances = [variances[0]] + [to_share(variances[k], k) for k in range(1, shares)]

    edge = array(exp_count * SENT, col_count)
    near, far = call(edges_kernel, "edges", [edge, edge], warped)
    near = lax.ppermute(near, "sky", [(i, i ^ 1) for i in range(sky_count) if i ^ 1 < sky_count])
    partner = {i: i + 1 if i % 2 else i - 1 for i in range(1, sky_count)}
    pairs = []
    for i in range(sky_count):
        j = partner.get(i, i)
        ends = j in (i, sky_count)
        for e in range(shares):
            pairs.append((i * shares + e, i * shares + (e + 1) % shares if ends else j * shares + e))
    far = lax.ppermute(far, ("sky", "exp"), pairs)

    inner_band, outer_band, col_band, active, covered, inner_features, outer_features = call(
        functools.partial(setup_kernel, total_rows),
        "setup",
        [
            array(basis_count, size, LANES),
            array(basis_count, 2 * EDGE, LANES),
            array(basis_count, LANES, LANES),
            array(exp_count, pair_count, 8, LANES, dtype=F32),
            array(exp_count, row_count, LANES, dtype=F32),
            array(2 * size, LANES),
            array(4 * EDGE, LANES),
        ],
        basis_taps,
        jnp.transpose(coeffs, (1, 0, 2)),
        degrees,
        footprint,
        masks,
        cost=0.5,
    )

    def first(k):
        return call(
            functools.partial(first_kernel, k, shares, half),
            "first",
            [array(exp_count, inner, width), array(exp_count, pair_count, 8 * PIECES, spans)],
            warped,
            active,
            covered,
            inner_features,
            inner_band,
            col_band,
            scratch=[
                pltpu.VMEM((exp_count, LANES, spans), BF16),
                pltpu.VMEM((exp_count, basis_count * size, spans), BF16),
            ],
            mebibytes=12,
            cost=0.01 if k else 1.5,
        )

    def second(k, near, far, lines):
        return call(
            functools.partial(second_kernel, k, shares, half),
            "second",
            array(exp_count, 2 * EDGE, width),
            warped,
            near,
            far,
            covered,
            outer_features,
            outer_band,
            col_band,
            lines,
            scratch=[
                pltpu.VMEM((exp_count, LANES, spans), BF16),
                pltpu.VMEM((exp_count, basis_count * 2 * EDGE, spans), BF16),
            ],
            mebibytes=12,
            cost=0.01,
        )

    inner_features, near = lax.optimization_barrier((inner_features, near))
    firsts, seconds = [None] * shares, [None] * shares
    held = [None] * shares
    for k in range(1, shares):
        firsts[k], held[k] = first(k)
        firsts[k] = to_share(firsts[k], k)
    firsts[0], held[0] = first(0)
    variances, near, firsts[0] = lax.optimization_barrier((variances, near, firsts[0]))
    for k in range(1, shares):
        seconds[k] = second(k, near, far, held[k])
    seconds[1:], held[0] = lax.optimization_barrier((seconds[1:], held[0]))
    seconds[1:] = [to_share(seconds[k], k) for k in range(1, shares)]
    seconds[0] = second(0, near, far, held[0])

    done = call(
        functools.partial(first_coadd_kernel, shares),
        "first_coadd",
        array(inner, width, dtype=F32),
        *firsts,
        *variances,
        cost=0.01,
    )
    return pl.pallas_call(
        functools.partial(second_coadd_kernel, shares),
        out_shape=array(row_count, width, dtype=F32),
        in_specs=[vmem] * (2 * shares + 1),
        out_specs=pl.BlockSpec(memory_space=pl.ANY),
        scratch_shapes=[pltpu.VMEM((2 * EDGE, width), F32), pltpu.SemaphoreType.DMA((3,))],
        compiler_params=pltpu.CompilerParams(vmem_limit_bytes=8 * 2**20),
        name="second_coadd",
    )(*seconds, *variances, done)


def solution(mesh):
    in_specs = (
        P("exp", "sky", None),
        P("exp", "sky", None),
        P(),
        P("exp", None, None),
        P("exp", None),
        P("exp", None),
        P("exp", "sky"),
    )
    return jax.shard_map(body, mesh=mesh, in_specs=in_specs, out_specs=P("sky", "exp"), check_vma=False)
```

```python
import functools

import jax
import jax.numpy as jnp
from jax import lax
from jax.experimental import pallas as pl
from jax.experimental.pallas import tpu as pltpu
from jax.sharding import PartitionSpec as P

POWERS = ((0, 0), (1, 0), (0, 1), (2, 0), (1, 1), (0, 2), (3, 0), (2, 1), (1, 2), (0, 3))
TERM = {power: index for index, power in enumerate(POWERS)}
ROWS_PER_WORD = 15
EDGE = 16
SENT = 12
LANES = 128
GROUP = 5
PIECES = 6
F32 = jnp.float32
BF16 = jnp.bfloat16


def round_up(value, unit):
    return -(-value // unit) * unit


def segments(width, tap_count):
    valid = LANES - tap_count + 1
    return [(at, min(valid, width - at)) for at in range(0, width, valid)]


def share_start(k, shares, width):
    return pl.multiple_of(lax.rem(lax.axis_index("exp") + k, shares) * width, LANES)


def variance_kernel(variance, *parts):
    shares, width = len(parts), parts[0].shape[2]
    for k in range(shares):
        parts[k][...] = variance[:, :, pl.ds(share_start(k, shares, width), width)]


def edges_kernel(warped, near, far):
    exp_count, row_count, _ = warped.shape
    even = lax.rem(lax.axis_index("sky"), 2) == 0
    heads, tails = [], []
    for e in range(exp_count):
        image = warped[e].astype(F32)
        heads.append(image[:SENT])
        tails.append(image[row_count - SENT :])
    head, tail = jnp.concatenate(heads, axis=0), jnp.concatenate(tails, axis=0)
    near[...] = jnp.where(even, tail, head).astype(BF16)
    far[...] = jnp.where(even, head, tail).astype(BF16)


def pieces(value):
    high = value.astype(BF16).astype(F32)
    rest = value - high
    middle = rest.astype(BF16).astype(F32)
    return high, middle, rest - middle


def row_features(first, size, total_rows):
    u = row_position(first, size, total_rows)
    lane = lax.broadcasted_iota(jnp.int32, u.shape, 1)
    power, group = (lane >> 1) & 3, lane >> 3
    value = jnp.where(power == 0, 1.0, jnp.where(power == 1, u, jnp.where(power == 2, u * u, u * u * u)))
    high, middle, low = pieces(value)
    value = jnp.where((group == 1) | (group == 4), middle, jnp.where(group == 2, low, high))
    value = jnp.where(group < PIECES, value, 0.0)
    odd = (lane & 1) == 1
    return jnp.where(odd, 0.0, value).astype(BF16), jnp.where(odd, value, 0.0).astype(BF16)


def setup_kernel(
    total_rows, taps, coeffs, degrees, footprint, masks,
    inner_band, outer_band, col_band, active, covered, inner_features, outer_features
):
    basis_count, _, tap_count = taps.shape
    exp_count, row_count, _ = covered.shape
    half = tap_count // 2
    inner = inner_band.shape[1]

    both = jnp.concatenate([taps[b].astype(F32) for b in range(basis_count)], axis=0)
    lines = jnp.concatenate([both, jnp.zeros((2 * basis_count, LANES - tap_count), F32)], axis=1).astype(BF16)
    lane = lax.broadcasted_iota(jnp.int32, (LANES, LANES), 1)
    tap = lax.broadcasted_iota(jnp.int32, (LANES, LANES), 0)
    flip = (lane + tap == LANES).astype(F32) + ((lane == 0) & (tap == 0)).astype(F32)
    flipped = jnp.dot(lines, flip.astype(BF16), preferred_element_type=F32)
    lines = lines.astype(F32)

    def circulant(line, size):
        return pltpu.roll(jnp.broadcast_to(line, (size, LANES)), 0, 1, stride=1, stride_axis=0)

    near = pltpu.roll(lines, EDGE - half, 1)
    far = pltpu.roll(lines, LANES - 2 * EDGE - half, 1)
    for b in range(basis_count):
        upper = circulant(near[2 * b : 2 * b + 1], inner)
        lower = circulant(far[2 * b : 2 * b + 1], EDGE)
        inner_band[b] = upper.astype(BF16)
        outer_band[b] = jnp.concatenate([upper[:EDGE], lower], axis=0).astype(BF16)
        col_band[b] = circulant(flipped[2 * b + 1 : 2 * b + 2], LANES).astype(BF16)

    term_count = coeffs.shape[2]
    term = lax.broadcasted_iota(jnp.int32, (1, term_count), 1)
    order = jnp.zeros((1, term_count), F32)
    for index, (p, q) in enumerate(POWERS):
        order = jnp.where(term == index, float(p + q), order)
    wide = jnp.concatenate([degrees[...].astype(F32), jnp.zeros((exp_count, LANES - basis_count), F32)], axis=1)
    by_basis = jnp.concatenate([wide, jnp.zeros((8 - exp_count, LANES), F32)], axis=0).T
    local = lax.broadcasted_iota(jnp.int32, (row_count, LANES), 0)
    total = local + lax.axis_index("sky") * row_count
    for e in range(exp_count):
        own = jnp.concatenate([coeffs[b, e : e + 1, :] for b in range(basis_count)], axis=0)
        kept = jnp.where(order <= by_basis[:basis_count, e : e + 1], own, 0.0)
        kept = jnp.concatenate([kept, jnp.zeros((16 - basis_count, term_count), F32)], axis=0)
        kept = jnp.concatenate([kept, jnp.zeros((16, LANES - term_count), F32)], axis=1)
        place = lax.broadcasted_iota(jnp.int32, kept.shape, 1)
        powers = []
        for p in range(4):
            value = jnp.zeros_like(kept)
            for q in range(4 - p):
                value = jnp.where(place == q, pltpu.roll(kept, (q - TERM[p, q]) % LANES, 1), value)
            powers.append(value)
        for pair in range(active.shape[1]):
            active[e, pair] = jnp.concatenate([value[2 * pair : 2 * pair + 2] for value in powers], axis=0)
        word = jnp.broadcast_to(masks[e : e + 1, 0:1], (row_count, LANES))
        first = jnp.zeros((row_count, LANES), jnp.int32)
        for w in range(1, masks.shape[1]):
            here = local >= w * ROWS_PER_WORD
            word = jnp.where(here, jnp.broadcast_to(masks[e : e + 1, w : w + 1], (row_count, LANES)), word)
            first = jnp.where(here, w * ROWS_PER_WORD, first)
        planes = lax.shift_right_logical(word, 2 * (local - first)) & 3
        low = jnp.broadcast_to(footprint[e : e + 1, 0:1], (row_count, LANES))
        high = jnp.broadcast_to(footprint[e : e + 1, 1:2], (row_count, LANES))
        covered[e] = ((total >= low) & (total < high) & (planes != 3)).astype(F32)
    top = lax.axis_index("sky") * row_count
    for odd, value in enumerate(row_features(top + EDGE, inner, total_rows)):
        inner_features[odd * inner : (odd + 1) * inner] = value
    upper = row_features(top, EDGE, total_rows)
    lower = row_features(top + row_count - EDGE, EDGE, total_rows)
    for odd in range(2):
        outer_features[2 * EDGE * odd : 2 * EDGE * (odd + 1)] = jnp.concatenate([upper[odd], lower[odd]], axis=0)


def windows_of(read, start, width, col_count, parts, half):
    left_at = pl.multiple_of(jnp.maximum(start - LANES, 0), LANES)
    right_at = pl.multiple_of(jnp.minimum(start + width, col_count - LANES), LANES)
    left = jnp.where(start > 0, read(left_at, LANES), 0.0)
    right = jnp.where(start + width < col_count, read(right_at, LANES), 0.0)
    middle = read(start, width)
    blocks = [left] + [middle[:, at : at + LANES] for at in range(0, width, LANES)] + [right]
    blocks = [pltpu.roll(block, half, 1) for block in blocks]
    lane = lax.broadcasted_iota(jnp.int32, left.shape, 1)
    place = jnp.where(lane >= half, lane - half, lane - half + LANES)
    pieces = []
    for at, _ in parts:
        base, offset = divmod(LANES + at - half, LANES)
        pieces.append(jnp.where(place >= offset, blocks[base], blocks[base + 1]))
    return jnp.concatenate(pieces, axis=1).astype(BF16)


def line_polynomials(active, lines, start, parts, col_count):
    exp_count, pair_count, rows, _ = active.shape
    lane = lax.broadcasted_iota(jnp.int32, (rows, LANES), 1)
    for s, (at, _) in enumerate(parts):
        col_at = at + jnp.where(lane >= at % LANES, lane - at % LANES, lane - at % LANES + LANES)
        v = (2.0 * (start + col_at).astype(F32) + 1.0) / col_count - 1.0
        span = slice(s * LANES, (s + 1) * LANES)
        for e in range(exp_count):
            for pair in range(pair_count):
                values = active[e, pair]
                c0, c1, c2, c3 = (jnp.broadcast_to(values[:, q : q + 1], values.shape) for q in range(4))
                high, middle, low = pieces(c0 + v * (c1 + v * (c2 + v * c3)))
                lines[e, pair, 0:16, span] = jnp.concatenate([high, high], axis=0).astype(BF16)
                lines[e, pair, 16:32, span] = jnp.concatenate([high, middle], axis=0).astype(BF16)
                lines[e, pair, 32:48, span] = jnp.concatenate([middle, low], axis=0).astype(BF16)


def weighted_sums(members, lines, features, rows, col_band, size):
    spans = [slice(s * LANES, (s + 1) * LANES) for _, s in members]
    exposures = sorted({e for e, _ in members})
    totals = [None] * len(members)
    for b in range(col_band.shape[0]):
        odd = b % 2
        if not odd:
            fields = {}
            for e in exposures:
                own = [s for other, s in members if other == e]
                columns = lines[e, b // 2, :, own[0] * LANES : (own[-1] + 1) * LANES]
                product = jnp.dot(features[:, : 8 * PIECES], columns, preferred_element_type=F32)
                for i, s in enumerate(own):
                    fields[e, s] = product[:, i * LANES : (i + 1) * LANES]
        window = jnp.concatenate(
            [rows[e, b * size : (b + 1) * size, span] for (e, _), span in zip(members, spans)], axis=0
        )
        along = jnp.dot(window, col_band[b], preferred_element_type=F32)
        for i, member in enumerate(members):
            value = fields[member][odd * size : (odd + 1) * size] * along[i * size : (i + 1) * size]
            totals[i] = value if b == 0 else totals[i] + value
    return totals


def joined(blocks, parts, width):
    out = []
    for low in range(0, width, LANES):
        lane = low + lax.broadcasted_iota(jnp.int32, blocks[0].shape, 1)
        tile = None
        for block, (at, size) in zip(blocks, parts):
            if at < low + LANES and at + size > low:
                tile = block if tile is None else jnp.where(lane >= at, block, tile)
        out.append(tile)
    return jnp.concatenate(out, axis=1)


def row_position(first, rows, total_rows):
    row_at = first + lax.broadcasted_iota(jnp.int32, (rows, LANES), 0)
    return (2.0 * row_at.astype(F32) + 1.0) / total_rows - 1.0


def first_kernel(
    k, shares, half, warped, active, covered, features, inner_band, col_band, matched, lines, strip, rows
):
    exp_count, row_count, col_count = warped.shape
    basis_count, size, _ = inner_band.shape
    _, inner, width = matched.shape
    parts = segments(width, 2 * half + 1)
    start = share_start(k, shares, width)
    line_polynomials(active, lines, start, parts, col_count)
    band = inner_band[...].reshape(basis_count * size, LANES)
    for e in range(exp_count):

        def read(at, count):
            own = warped[e, :, pl.ds(at, count)].astype(F32)
            return jnp.concatenate([own, jnp.zeros((LANES - row_count, count), F32)], axis=0)

        strip[e] = windows_of(read, start, width, col_count, parts, half)
        rows[e] = jnp.dot(band, strip[e], preferred_element_type=F32).astype(BF16)
    for e in range(exp_count):
        blocks = []
        for low in range(0, len(parts), GROUP):
            members = [(e, s) for s in range(low, min(low + GROUP, len(parts)))]
            blocks += weighted_sums(members, lines, features, rows, col_band, size)
        counts = jnp.concatenate([covered[e, EDGE : EDGE + inner]] * (width // LANES), axis=1) > 0
        matched[e] = jnp.where(counts, joined(blocks, parts, width)[:inner], jnp.inf).astype(BF16)


def second_kernel(
    k, shares, half, warped, near, far, covered, features, outer_band, col_band, lines, matched, strip, rows
):
    exp_count, row_count, col_count = warped.shape
    basis_count, size, _ = outer_band.shape
    width = matched.shape[2]
    parts = segments(width, 2 * half + 1)
    span = LANES // 2 - EDGE
    sky = lax.axis_index("sky")
    even = lax.rem(sky, 2) == 0
    start = share_start(k, shares, width)
    band = outer_band[...].reshape(basis_count * size, LANES)
    for e in range(exp_count):

        def read(at, count):
            own = warped[e, :, pl.ds(at, count)].astype(F32)
            same = near[:, pl.ds(at, count)].astype(F32)[e * SENT : (e + 1) * SENT]
            other = far[:, pl.ds(at, count)].astype(F32)[e * SENT : (e + 1) * SENT]
            up, down = jnp.where(even, other, same), jnp.where(even, same, other)
            up = jnp.where(sky > 0, up, 0.0)
            down = jnp.where(sky < lax.axis_size("sky") - 1, down, 0.0)
            gap = jnp.zeros((EDGE - SENT, count), F32)
            return jnp.concatenate([gap, up, own[:span], own[row_count - span :], down, gap], axis=0)

        strip[e] = windows_of(read, start, width, col_count, parts, half)
        rows[e] = jnp.dot(band, strip[e], preferred_element_type=F32).astype(BF16)
    members = [(e, s) for e in range(exp_count) for s in range(len(parts))]
    every = weighted_sums(members, lines, features, rows, col_band, size)
    for e in range(exp_count):
        blocks = every[e * len(parts) : (e + 1) * len(parts)]
        counts = jnp.concatenate([covered[e, :EDGE], covered[e, row_count - EDGE :]], axis=0)
        counts = jnp.concatenate([counts] * (width // LANES), axis=1) > 0
        matched[e] = jnp.where(counts, joined(blocks, parts, width), jnp.inf).astype(BF16)


def robust_sum(fields, spreads):
    values, variances, weights = [], [], []
    for value, spread in zip(fields, spreads):
        counts = value < jnp.inf
        spread = jnp.where(counts, spread, jnp.inf)
        values.append(jnp.where(counts, value, 0.0))
        variances.append(spread)
        weights.append(1.0 / spread)
    first = sum(w * x for w, x in zip(weights, values)) / (1.0 + sum(weights))
    robust = [1.0 / (s + (x - first) * (x - first) * (1.0 / 9.0)) for s, x in zip(variances, values)]
    return sum(r * x for r, x in zip(robust, values)) / (1.0 + sum(robust))


def first_coadd_kernel(shares, *refs):
    fields, variances, coadd = refs[:shares], refs[shares : 2 * shares], refs[-1]
    exp_count, size, width = fields[0].shape
    pairs = [(k, e) for k in range(shares) for e in range(exp_count)]
    for at in range(0, width, LANES):
        span = slice(at, at + LANES)
        values = [fields[k][e, :, span].astype(F32) for k, e in pairs]
        spreads = [variances[k][e, :, span].astype(F32)[EDGE : EDGE + size] for k, e in pairs]
        coadd[:, span] = robust_sum(values, spreads)


def second_coadd_kernel(shares, *refs):
    fields, variances, done = refs[:shares], refs[shares : 2 * shares], refs[2 * shares]
    coadd, edges, copied = refs[2 * shares + 1 :]
    exp_count, row_count, width = variances[0].shape
    size = done.shape[0]
    pairs = [(k, e) for k in range(shares) for e in range(exp_count)]
    inner = pltpu.make_async_copy(done, coadd.at[EDGE : EDGE + size], copied.at[0])
    inner.start()
    for at in range(0, width, LANES):
        span = slice(at, at + LANES)
        values = [fields[k][e, :, span].astype(F32) for k, e in pairs]
        spreads = []
        for k, e in pairs:
            spread = variances[k][e, :, span].astype(F32)
            spreads.append(jnp.concatenate([spread[:EDGE], spread[row_count - EDGE :]], axis=0))
        edges[:, span] = robust_sum(values, spreads)
    upper = pltpu.make_async_copy(edges.at[:EDGE], coadd.at[:EDGE], copied.at[1])
    lower = pltpu.make_async_copy(edges.at[EDGE:], coadd.at[row_count - EDGE :], copied.at[2])
    upper.start()
    lower.start()
    inner.wait()
    upper.wait()
    lower.wait()


def body(warped, variance, basis_taps, coeffs, degrees, footprint, masks):
    exp_count, row_count, col_count = warped.shape
    basis_count, _, tap_count = basis_taps.shape
    half = tap_count // 2
    sky_count, shares = lax.axis_size("sky"), lax.axis_size("exp")
    width = col_count // shares
    total_rows = row_count * sky_count
    inner = row_count - 2 * EDGE
    size = round_up(inner, 16)
    pair_count = -(-basis_count // 2)
    spans = len(segments(width, tap_count)) * LANES
    vmem = pl.BlockSpec(memory_space=pltpu.VMEM)

    def array(*shape, dtype=BF16):
        return jax.ShapeDtypeStruct(shape, dtype)

    def call(kernel, name, out_shape, *operands, scratch=(), mebibytes=8, cost=0.01):
        outputs = len(out_shape) if isinstance(out_shape, list) else 0
        return pl.pallas_call(
            kernel,
            out_shape=out_shape,
            in_specs=[vmem] * len(operands),
            out_specs=[vmem] * outputs if outputs else vmem,
            scratch_shapes=scratch,
            compiler_params=pltpu.CompilerParams(vmem_limit_bytes=mebibytes * 2**20),
            cost_estimate=pl.CostEstimate(flops=int(cost * 1e9), bytes_accessed=int(cost * 3e6), transcendentals=0),
            name=name,
        )(*operands)

    def to_share(values, k):
        return lax.ppermute(values, "exp", [(i, (i + k) % shares) for i in range(shares)])

    variances = call(variance_kernel, "variance", [array(exp_count, row_count, width)] * shares, variance)
    variances = [variances[0]] + [to_share(variances[k], k) for k in range(1, shares)]

    edge = array(exp_count * SENT, col_count)
    near, far = call(edges_kernel, "edges", [edge, edge], warped)
    near = lax.ppermute(near, "sky", [(i, i ^ 1) for i in range(sky_count) if i ^ 1 < sky_count])
    partner = {i: i + 1 if i % 2 else i - 1 for i in range(1, sky_count)}
    pairs = []
    for i in range(sky_count):
        j = partner.get(i, i)
        ends = j in (i, sky_count)
        for e in range(shares):
            pairs.append((i * shares + e, i * shares + (e + 1) % shares if ends else j * shares + e))
    far = lax.ppermute(far, ("sky", "exp"), pairs)

    inner_band, outer_band, col_band, active, covered, inner_features, outer_features = call(
        functools.partial(setup_kernel, total_rows),
        "setup",
        [
            array(basis_count, size, LANES),
            array(basis_count, 2 * EDGE, LANES),
            array(basis_count, LANES, LANES),
            array(exp_count, pair_count, 8, LANES, dtype=F32),
            array(exp_count, row_count, LANES, dtype=F32),
            array(2 * size, LANES),
            array(4 * EDGE, LANES),
        ],
        basis_taps,
        jnp.transpose(coeffs, (1, 0, 2)),
        degrees,
        footprint,
        masks,
        cost=0.5,
    )

    def first(k):
        return call(
            functools.partial(first_kernel, k, shares, half),
            "first",
            [array(exp_count, inner, width), array(exp_count, pair_count, 8 * PIECES, spans)],
            warped,
            active,
            covered,
            inner_features,
            inner_band,
            col_band,
            scratch=[
                pltpu.VMEM((exp_count, LANES, spans), BF16),
                pltpu.VMEM((exp_count, basis_count * size, spans), BF16),
            ],
            mebibytes=12,
            cost=0.01 if k else 1.5,
        )

    def second(k, near, far, lines):
        return call(
            functools.partial(second_kernel, k, shares, half),
            "second",
            array(exp_count, 2 * EDGE, width),
            warped,
            near,
            far,
            covered,
            outer_features,
            outer_band,
            col_band,
            lines,
            scratch=[
                pltpu.VMEM((exp_count, LANES, spans), BF16),
                pltpu.VMEM((exp_count, basis_count * 2 * EDGE, spans), BF16),
            ],
            mebibytes=12,
            cost=0.01,
        )

    inner_features, near = lax.optimization_barrier((inner_features, near))
    firsts, seconds = [None] * shares, [None] * shares
    held = [None] * shares
    for k in range(1, shares):
        firsts[k], held[k] = first(k)
        firsts[k] = to_share(firsts[k], k)
    firsts[0], held[0] = first(0)
    variances, near, firsts[0] = lax.optimization_barrier((variances, near, firsts[0]))
    for k in range(1, shares):
        seconds[k] = second(k, near, far, held[k])
    seconds[1:], held[0] = lax.optimization_barrier((seconds[1:], held[0]))
    seconds[1:] = [to_share(seconds[k], k) for k in range(1, shares)]
    seconds[0] = second(0, near, far, held[0])

    done = call(
        functools.partial(first_coadd_kernel, shares),
        "first_coadd",
        array(inner, width, dtype=F32),
        *firsts,
        *variances,
        cost=0.01,
    )
    return pl.pallas_call(
        functools.partial(second_coadd_kernel, shares),
        out_shape=array(row_count, width, dtype=F32),
        in_specs=[vmem] * (2 * shares + 1),
        out_specs=pl.BlockSpec(memory_space=pl.ANY),
        scratch_shapes=[pltpu.VMEM((2 * EDGE, width), F32), pltpu.SemaphoreType.DMA((3,))],
        compiler_params=pltpu.CompilerParams(vmem_limit_bytes=8 * 2**20),
        name="second_coadd",
    )(*seconds, *variances, done)


def solution(mesh):
    in_specs = (
        P("exp", "sky", None),
        P("exp", "sky", None),
        P(),
        P("exp", None, None),
        P("exp", None),
        P("exp", None),
        P("exp", "sky"),
    )
    return jax.shard_map(body, mesh=mesh, in_specs=in_specs, out_specs=P("sky", "exp"), check_vma=False)
```
